32 devices in a mesh: mp: 4 (over y, core), rows: 8 (over z, x).
Axes of the slice: x: 2, y: 2, z: 4, core: 2. Of those that a mesh axis runs over, the one named last changes fastest.
Arguments:
- hidden: bfloat16 [256, 4096], P('rows'), may hold values from -60 to 60
- attn_gain: float32 [4096], replicated, may hold values from 0.3 to 1.7
- w_query: bfloat16 [4096, 4096], P(None, 'mp'), may hold values from -0.09375 to 0.09375
- w_key: bfloat16 [4096, 1024], P(None, 'mp'), may hold values from -0.09375 to 0.09375
- w_value: bfloat16 [4096, 1024], P(None, 'mp'), may hold values from -0.09375 to 0.09375
- w_output: bfloat16 [4096, 4096], P('mp'), may hold values from -0.09375 to 0.09375
- query_gain: float32 [128], replicated, may hold values from 0.5 to 1.5
- key_gain: float32 [128], replicated, may hold values from 0.5 to 1.5
- key_cache: bfloat16 [256, 32, 1024], P('rows', None, 'mp'), may hold values from -730 to 730
- value_cache: bfloat16 [256, 32, 1024], P('rows', None, 'mp'), may hold values from -6 to 6
- lengths: int32 [256], P('rows'), may hold values from 1 to 32
- final_gain: float32 [4096], replicated, may hold values from 0.4 to 1.6
- old_embed: bfloat16 [256, 4096], P('rows'), may hold values from -72 to 72
- slab: bfloat16 [4096, 4096], P('rows', 'mp'), may hold values from -6 to 6
- owners: int32 [4096, 1], P('rows'), may hold values from 0 to 7; in each aligned block of 512 rows (0 to 511, 512 to 1023, ...) at most 128 rows name the same one
Outputs:
- migrated: bfloat16 [8192, 4096], P('rows', 'mp')
The draws below stay inside these ranges and needn't reach their ends.
Inputs may be any that keep to these rules, and one draw needn't show every extreme that they name: `owners`: in each aligned block of 512 cache rows no owner is named by more than 128 rows.
All inputs are finite; a program needn't handle non-finite values.
Results may differ from the reference program's by a relative error of at most 0.008.
Values may be sent and summed in bfloat16 or wider, within the bound.
A program may use at most 128 MiB of HBM per device.

```python
import math
import jax
import jax.numpy as jnp
import numpy as np
from jax import lax

D = 4096
HEADS = 32
KV_HEADS = 8
HEAD = 128
CTX = 32
ITERS = 3
CACHE_DEV = 512
ANCHORS = 256
CACHE = 4096
CAP = 128
N_ROWS = 8


def draw_hidden(key, part):
    key_rows, key_cols, key_base = jax.random.split(key, 3)
    row_scale = jnp.exp(jax.random.uniform(key_rows, (ANCHORS, 1), minval=0.0, maxval=math.log(3.16)))
    col_scale = jnp.exp(jax.random.uniform(key_cols, (1, D), minval=0.0, maxval=math.log(3.16)))
    base = jnp.clip(jax.random.normal(key_base, (ANCHORS, D)), -6.0, 6.0)
    return (base * row_scale * col_scale).astype(jnp.bfloat16)


def draw_old_embed(key, part):
    key_rows, key_cols, key_base = jax.random.split(key, 3)
    row_scale = jnp.exp(jax.random.uniform(key_rows, (ANCHORS, 1), minval=0.0, maxval=math.log(2.0)))
    rising = 1.0 + 2.0 * jnp.arange(D, dtype=jnp.float32)[None, :] / D
    col_scale = rising * jnp.exp(jax.random.uniform(key_cols, (1, D), minval=0.0, maxval=math.log(2.0)))
    base = jnp.clip(jax.random.normal(key_base, (ANCHORS, D)), -6.0, 6.0)
    return (base * row_scale * col_scale).astype(jnp.bfloat16)


def draw_key_cache(key, part):
    key_base = jax.random.fold_in(key, 1)
    shape = (ANCHORS, CTX, KV_HEADS * HEAD)
    base = jnp.clip(jax.random.normal(key_base, shape), -6.0, 6.0)
    values = base
    return values.astype(jnp.bfloat16)


def touch_ends(drawn, rng, least, top_value):
    longest = drawn.shape.index(max(drawn.shape))
    spots = []
    for shift in (0, 1):
        where = [jax.random.randint(jax.random.fold_in(rng, axis), (), 0, length) for axis, length in enumerate(drawn.shape)]
        where[longest] = (where[longest] + shift) % drawn.shape[longest]
        spots.append(tuple(where))
    return drawn.at[spots[0]].set(least).at[spots[1]].set(top_value)


def level_of(rng, extent, cuts, least, high):
    def one(axis_at, blocks):
        draws = jax.random.uniform(jax.random.fold_in(jax.random.fold_in(rng, 6), axis_at), (blocks,), jnp.float32, least / len(cuts), high / len(cuts))
        return jnp.repeat(jnp.exp(draws), extent[axis_at] // blocks).reshape((-1,) + (1,) * (len(extent) - axis_at - 1))

    level = one(*cuts[0])
    for cut in cuts[1:]:
        level = level * one(*cut)
    return level


def deal_out(rng, own, number, rows, count, top, reach, lean):
    sequence = jax.random.permutation(rng, count)
    packed, usual = shares(count, rows * top, reach, lean, True), shares(count, rows * top, reach, lean, False)
    places = jnp.arange(count)

    def named(sizes, turn):
        used = int((sizes > 0).sum())
        fixed = max(1, used // 4)
        shifted = fixed + (places - fixed + turn * (used - fixed)) % max(1, count - fixed)
        return jnp.zeros((count,), jnp.int32).at[sequence[jnp.where(places < fixed, places, shifted)]].set(jnp.asarray(sizes, jnp.int32))

    sizes = jnp.where(number % 4 == 0, named(packed, number // 4), named(usual, number - number // 4 - 1))
    mixed = jax.random.permutation(jax.random.fold_in(own, 3), count)
    source_of, receiver = mixed[0:count // 2 * 2:2], mixed[1:count // 2 * 2:2]
    margin = jnp.minimum(sizes[source_of] - 1, reach - sizes[receiver]) // 2
    margin = jnp.where((source_of == sequence[0]) | (receiver == sequence[0]) | (sizes[receiver] == 0), 0, jnp.maximum(margin, 0))
    shifted = jax.random.randint(jax.random.fold_in(own, 4), (count // 2,), 0, 1 << 20) % (margin + 1)
    sizes = sizes.at[source_of].add(-shifted).at[receiver].add(shifted)
    labels = jnp.searchsorted(jnp.cumsum(sizes), jnp.arange(rows * top), side="right").astype(jnp.int32)
    table = labels.reshape(top, rows).T
    table = table[jax.random.permutation(jax.random.fold_in(own, 1), rows)]
    turn = jax.random.randint(jax.random.fold_in(own, 2), (rows, 1), 0, top)
    return jnp.take_along_axis(table, (jnp.arange(top)[None, :] + turn) % top, axis=1)


def shares(count, total, most, skew, full):
    weights = [(1 << 20) // math.isqrt(grade ** skew) + 1 for grade in range(1, count + 1)]
    largest = most if full else min(most, max(-(-total // count), total * weights[0] // sum(weights)))
    least = 1 if total - largest >= count - 1 else 0
    counts, spare = [largest] + [least] * (count - 1), total - largest - least * (count - 1)
    while spare > 0:
        movable = [i for i in range(1, count) if counts[i] < largest] or [i for i in range(1, count) if counts[i] < most]
        mass, remaining = sum([weights[i] for i in movable]), spare
        for i in movable:
            more = min(most - counts[i], max(1, remaining * weights[i] // mass), spare)
            counts[i] = counts[i] + more
            spare = spare - more
    return np.array(counts)


def bell_draw(stream_key, extent, spread, limit, shards=(), kind=jnp.bfloat16):
    drawn = spread * jax.random.normal(stream_key, extent, jnp.float32)
    if shards:
        drawn = drawn * level_of(stream_key, extent, shards, -0.22, 0.18)
    return jnp.clip(drawn, -limit, limit).astype(kind)


def setup_inputs(seed: int = 0) -> dict:
    keys = jax.random.split(jax.random.key(seed), 16)
    hidden = draw_hidden(jax.random.fold_in(keys[15], 71), 0)
    attn_gain = jnp.clip(jax.random.uniform(keys[1], (D,), jnp.float32, 0.3, 1.7), 0.3, 1.7)
    w_query = bell_draw(keys[2], (D, HEADS * HEAD), D ** -0.5, 0.09375, ((1, 4),))
    w_key = bell_draw(keys[3], (D, KV_HEADS * HEAD), D ** -0.5, 0.09375, ((1, 4),))
    w_value = bell_draw(keys[4], (D, KV_HEADS * HEAD), D ** -0.5, 0.09375, ((1, 4),))
    w_output = bell_draw(keys[5], (HEADS * HEAD, D), (HEADS * HEAD) ** -0.5, 0.09375, ((0, 4),))
    query_gain = jnp.clip(jax.random.uniform(keys[6], (HEAD,), jnp.float32, 0.5, 1.5), 0.5, 1.5)
    key_gain = jnp.clip(jax.random.uniform(keys[7], (HEAD,), jnp.float32, 0.5, 1.5), 0.5, 1.5)
    key_cache = draw_key_cache(jax.random.fold_in(keys[15], 71), 0)
    value_cache = bell_draw(keys[9], (ANCHORS, CTX, KV_HEADS * HEAD), 1.0, 6.0, ((0, 8), (2, 4)))
    lengths = touch_ends(jax.random.randint(keys[10], (ANCHORS,), 1, CTX + 1), jax.random.fold_in(keys[10], 1), 1, CTX).astype(jnp.int32)
    final_gain = jnp.clip(jax.random.uniform(keys[11], (D,), jnp.float32, 0.4, 1.6), 0.4, 1.6)
    old_embed = draw_old_embed(jax.random.fold_in(keys[15], 71), 0)
    slab = bell_draw(keys[13], (CACHE, D), 1.0, 6.0, ((0, 8), (1, 4)))
    owners_keys = jax.random.split(jax.random.fold_in(keys[14], 1), CACHE // CACHE_DEV)
    owners_turns = jax.random.permutation(jax.random.fold_in(keys[14], 3), CACHE // CACHE_DEV)
    owners = jax.vmap(lambda own, number: deal_out(jax.random.fold_in(keys[14], 2), own, number, CACHE_DEV, N_ROWS, 1, CAP, 2))(owners_keys, owners_turns).reshape((CACHE, 1))
    return {"hidden": hidden, "attn_gain": attn_gain, "w_query": w_query, "w_key": w_key, "w_value": w_value, "w_output": w_output, "query_gain": query_gain, "key_gain": key_gain, "key_cache": key_cache, "value_cache": value_cache, "lengths": lengths, "final_gain": final_gain, "old_embed": old_embed, "slab": slab, "owners": owners}


def rotate(values, position):
    half_width = values.shape[-1] // 2
    exponent = 2.0 * jnp.arange(half_width, dtype=jnp.float32) / values.shape[-1]
    frequency = jnp.exp(-exponent * math.log(1000000.0))
    angle = position[:, None, None] * frequency[None, None, :]
    cosine = jnp.cos(angle)
    sine = jnp.sin(angle)
    first = values[..., :half_width]
    second = values[..., half_width:]
    return jnp.concatenate([first * cosine - second * sine, second * cosine + first * sine], axis=-1)

def head_norm(values, gain):
    scale = lax.rsqrt(lax.optimization_barrier(jnp.mean(values * values, axis=-1, keepdims=True)) + 1e-06)
    return values * scale * gain

def reference(hidden, attn_gain, w_query, w_key, w_value, w_output, query_gain, key_gain, key_cache, value_cache, lengths, final_gain, old_embed, slab, owners):
    anchors = hidden.shape[0]
    group = HEADS // KV_HEADS
    hidden32 = hidden.astype(jnp.float32)
    normed = (hidden32 * lax.rsqrt(lax.optimization_barrier(jnp.mean(hidden32 * hidden32, axis=-1, keepdims=True)) + 1e-06) * attn_gain).astype(jnp.bfloat16)
    position = lengths.astype(jnp.float32)
    query = jnp.dot(normed, w_query, preferred_element_type=jnp.float32).reshape(anchors, HEADS, HEAD)
    query = rotate(head_norm(query, query_gain), position).astype(jnp.bfloat16)
    key_new = jnp.dot(normed, w_key, preferred_element_type=jnp.float32).reshape(anchors, KV_HEADS, HEAD)
    key_new = rotate(head_norm(key_new, key_gain), position).astype(jnp.bfloat16)
    value_new = jnp.dot(normed, w_value, preferred_element_type=jnp.float32).reshape(anchors, KV_HEADS, HEAD).astype(jnp.bfloat16)
    query32 = query.reshape(anchors, KV_HEADS, group, HEAD).astype(jnp.float32)
    keys32 = key_cache.reshape(anchors, CTX, KV_HEADS, HEAD).astype(jnp.float32)
    values32 = value_cache.reshape(anchors, CTX, KV_HEADS, HEAD).astype(jnp.float32)
    scale = 1.0 / math.sqrt(HEAD)
    scores = jnp.einsum('akgd,apkd->akgp', query32, keys32) * scale
    own_score = jnp.einsum('akgd,akd->akg', query32, key_new.astype(jnp.float32)) * scale
    valid = jnp.arange(CTX, dtype=jnp.int32)[None, :] < lengths[:, None]
    scores = jnp.where(valid[:, None, None, :], scores, -jnp.inf)
    top = jnp.maximum(lax.optimization_barrier(jnp.max(scores, axis=-1)), own_score)
    expo = jnp.exp(scores - top[..., None])
    own_expo = jnp.exp(own_score - top)
    total = lax.optimization_barrier(jnp.sum(expo, axis=-1)) + own_expo
    weights = (expo / total[..., None]).astype(jnp.bfloat16)
    own_weight = (own_expo / total).astype(jnp.bfloat16)
    attended = jnp.einsum('akgp,apkd->akgd', weights.astype(jnp.float32), values32)
    attended = attended + own_weight.astype(jnp.float32)[..., None] * value_new.astype(jnp.float32)[:, :, None, :]
    attended = attended.reshape(anchors, HEADS * HEAD).astype(jnp.bfloat16)
    state = hidden32 + jnp.dot(attended, w_output, preferred_element_type=jnp.float32)
    new_embed = (state * lax.rsqrt(lax.optimization_barrier(jnp.mean(state * state, axis=-1, keepdims=True)) + 1e-06) * final_gain).astype(jnp.bfloat16)
    cross = jnp.dot(old_embed.T, new_embed, preferred_element_type=jnp.float32)
    ridge = 0.125 * D
    highest = lax.Precision.HIGHEST
    old32 = old_embed.astype(jnp.float32)
    ridge_map = jnp.zeros_like(cross)
    residual = cross
    direction = cross
    res_sq = lax.optimization_barrier(jnp.sum(residual * residual, axis=0))
    for sweep in range(ITERS):
        image_docs = jnp.dot(old32, direction, precision=highest)
        curvature = lax.optimization_barrier(jnp.sum(image_docs * image_docs, axis=0)) + ridge * lax.optimization_barrier(jnp.sum(direction * direction, axis=0))
        alpha = res_sq / curvature
        ridge_map = ridge_map + alpha * direction
        image = jnp.dot(old32.T, image_docs, precision=highest) + ridge * direction
        residual = residual - alpha * image
        new_sq = lax.optimization_barrier(jnp.sum(residual * residual, axis=0))
        direction = residual + new_sq / res_sq * direction
        res_sq = new_sq
    map_b = ridge_map.astype(jnp.bfloat16)
    moved = jnp.dot(slab.astype(jnp.float32), map_b.astype(jnp.float32), preferred_element_type=jnp.float32).astype(jnp.bfloat16)
    owner_ids = owners[:, 0].reshape(N_ROWS, CACHE_DEV)
    onehot = (owner_ids[:, :, None] == jnp.arange(N_ROWS, dtype=jnp.int32)[None, None, :]).astype(jnp.int32)
    counted = jnp.cumsum(onehot, axis=1)
    slot = lax.optimization_barrier(jnp.sum((counted - 1) * onehot, axis=-1))
    source = jnp.arange(N_ROWS, dtype=jnp.int32)[:, None]
    target = ((owner_ids * N_ROWS + source) * CAP + slot).reshape(-1).astype(jnp.int32)
    migrated = jnp.zeros((N_ROWS * N_ROWS * CAP, D), jnp.bfloat16).at[target].set(moved)
    return migrated
```

```python
import functools
import math

import jax
import jax.numpy as jnp
from jax import lax
from jax.experimental import pallas as pl
from jax.experimental.pallas import tpu as pltpu
from jax.sharding import PartitionSpec as P

D = 4096
HEADS = 32
KV_HEADS = 8
HEAD = 128
ITERS = 3
MESH = pl.DeviceIdType.MESH
F32 = jnp.float32
BF16 = jnp.bfloat16
CHUNKS = 8


def dot(left, right, left_dim=1, right_dim=0):
    return lax.dot_general(
        left, right, (((left_dim,), (right_dim,)), ((), ())), preferred_element_type=F32
    )


def encode_kernel(
    n_mp, n_rows,
    hidden, attn_gain, w_query, w_key, w_value, w_output, query_gain, key_gain,
    key_cache, value_cache, lengths, final_gain, old_embed, slab, owners,
    new_out, gram_out, routed_out,
    wq, wk, wv, wo, kc, vc, sl, normed, q_acc, k_acc, v_acc, attended,
    part, part_in, part_sum, part_far, sq_own, sq_in, new_all,
    old_all, side, side_in, side_sum, side_far, outgoing, routed, gram,
    load_sem, weight_sem, wo_sem,
    part_a, part_b, sq_sem, new_f, new_n, old_f, old_n, side_a, side_b,
    trip_sem, gram_f, gram_n, routed_f, routed_n, out_sem,
):
    mp = lax.axis_index("mp")
    row = lax.axis_index("rows")
    docs, width = hidden.shape
    cols = width // n_mp
    anchors = n_rows * docs
    share = anchors // n_mp
    slab_rows = slab.shape[0]
    cap = outgoing.shape[2]
    kv_local = k_acc.shape[1] // HEAD
    group = HEADS // KV_HEADS
    ctx = key_cache.shape[0] // docs
    mp_half, rows_half = n_mp // 2, n_rows // 2
    mp_slow, core = mp // 2, mp % 2
    row_slow, row_fast = row // 2, row % 2

    def remote(src, dst, sems, spot, to_mp, to_row):
        return pltpu.make_async_remote_copy(
            src_ref=src, dst_ref=dst, send_sem=sems.at[0, spot], recv_sem=sems.at[1, spot],
            device_id={"mp": to_mp, "rows": to_row}, device_id_type=MESH,
        )

    def far_rows(buf, sems):
        return [
            remote(buf.at[row], buf.at[row], sems, off - 1, mp,
                   ((row_slow + off) % rows_half) * 2 + row_fast)
            for off in range(1, rows_half)
        ]

    def near_rows(buf, sems):
        found = []
        for off in range(rows_half):
            block = ((row_slow + rows_half - off) % rows_half) * 2 + row_fast
            found.append(remote(buf.at[block], buf.at[block], sems, off, mp,
                                row_slow * 2 + 1 - row_fast))
        return found

    def far_mp(buf, sems):
        return [
            remote(buf.at[mp], buf.at[mp], sems, off - 1,
                   ((mp_slow + off) % mp_half) * 2 + core, row)
            for off in range(1, mp_half)
        ]

    def near_mp(buf, sems):
        found = []
        for off in range(mp_half):
            block = ((mp_slow + mp_half - off) % mp_half) * 2 + core
            found.append(remote(buf.at[block], buf.at[block], sems, off,
                                mp_slow * 2 + 1 - core, row))
        return found

    def reduce_far(summed, landed, sems):
        found = []
        for off in range(1, mp_half):
            there = (mp_slow + off) % mp_half
            found.append(remote(summed.at[there], landed.at[off - 1], sems, off - 1,
                                there * 2 + core, row))
        return found

    def start(copies):
        for copy in copies:
            copy.start()

    sent = []

    def received(copies):
        for copy in copies:
            copy.wait_recv()
            sent.append(copy)

    depth = width // CHUNKS

    def weight_copies(step):
        span = pl.ds(pl.multiple_of(step * depth, depth), depth)
        return [
            pltpu.make_async_copy(src.at[span, :], dst.at[span, :], weight_sem.at[i, step])
            for i, (src, dst) in enumerate(((w_query, wq), (w_key, wk), (w_value, wv)))
        ]

    def output_block(step):
        return 2 * (step % mp_half) + lax.rem(core + 1 + step // mp_half, 2)

    def output_copy(step):
        span = pl.ds(pl.multiple_of(output_block(step) * cols, cols), cols)
        return pltpu.make_async_copy(w_output.at[:, span], wo.at[:, span], wo_sem.at[step])

    for step in range(CHUNKS):
        start(weight_copies(step))
    loads = [
        pltpu.make_async_copy(key_cache, kc, load_sem.at[0]),
        pltpu.make_async_copy(value_cache, vc, load_sem.at[1]),
        pltpu.make_async_copy(slab, sl, load_sem.at[2]),
    ]
    start(loads)
    for step in range(n_mp):
        output_copy(step).start()

    barrier = pltpu.get_barrier_semaphore()
    for off in range(1, n_rows):
        pl.semaphore_signal(barrier, inc=1, device_id={"mp": mp, "rows": lax.rem(row + off, n_rows)},
                            device_id_type=MESH)
    for off in range(1, n_mp):
        pl.semaphore_signal(barrier, inc=1, device_id={"mp": lax.rem(mp + off, n_mp), "rows": row},
                            device_id_type=MESH)
    mine = pl.ds(pl.multiple_of(mp * cols, cols), cols)
    old_all[row] = old_embed[:, mine]
    pl.semaphore_wait(barrier, n_rows + n_mp - 2)

    old_far = far_rows(old_all, old_f)
    start(old_far)
    old_near = near_rows(old_all, old_n)
    old_near[0].start()

    hidden32 = hidden[...].astype(F32)
    normed[...] = (
        hidden32 * lax.rsqrt(jnp.mean(hidden32 * hidden32, axis=-1, keepdims=True) + 1e-06)
        * attn_gain[...]
    ).astype(BF16)

    q_acc[...] = jnp.zeros_like(q_acc)
    k_acc[...] = jnp.zeros_like(k_acc)
    v_acc[...] = jnp.zeros_like(v_acc)

    def project(step, carry):
        span = pl.ds(pl.multiple_of(step * depth, depth), depth)
        for copy in weight_copies(step):
            copy.wait()
        piece = normed[:, span]
        q_acc[...] += dot(piece, wq[span, :])
        k_acc[...] += dot(piece, wk[span, :])
        v_acc[...] += dot(piece, wv[span, :])
        return carry

    lax.fori_loop(0, CHUNKS, project, 0)

    tall = group * docs
    spot = lax.broadcasted_iota(jnp.int32, (tall, docs), 0) % docs
    named = lax.broadcasted_iota(jnp.int32, (tall, docs), 1)
    length = jnp.sum(
        jnp.where(spot == named, lengths[...].astype(F32), 0.0), axis=-1, keepdims=True
    )
    lane = lax.broadcasted_iota(jnp.int32, (docs, HEAD), 1)
    half = HEAD // 2
    frequency = jnp.exp(
        -(2.0 * (lane % half).astype(F32) / HEAD) * math.log(1000000.0)
    )
    angle = length[:docs] * frequency
    cosine = jnp.cos(angle)
    sine = jnp.sin(angle) * jnp.where(lane < half, -1.0, 1.0)

    def turned(values, gain):
        scale = lax.rsqrt(jnp.mean(values * values, axis=-1, keepdims=True) + 1e-06)
        values = values * scale * gain
        return (values * cosine + pltpu.roll(values, half, 1) * sine).astype(BF16)

    loads[0].wait()
    loads[1].wait()
    place_row = lax.broadcasted_iota(jnp.int32, (tall, docs * ctx), 0) % docs * ctx
    place_lane = lax.broadcasted_iota(jnp.int32, (tall, docs * ctx), 1)
    valid = (place_lane >= place_row) & (place_lane < place_row + length.astype(jnp.int32))
    for g in range(kv_local):
        span = slice(g * HEAD, (g + 1) * HEAD)
        queries = jnp.concatenate(
            [
                turned(q_acc[:, (g * group + h) * HEAD:(g * group + h + 1) * HEAD], query_gain[...])
                for h in range(group)
            ],
            axis=0,
        )
        key_new = jnp.concatenate([turned(k_acc[:, span], key_gain[...])] * group, axis=0)
        value_new = jnp.concatenate([v_acc[:, span].astype(BF16)] * group, axis=0)
        factor = 1.0 / math.sqrt(HEAD)
        scores = jnp.where(valid, dot(queries, kc[:, span], 1, 1) * factor, -jnp.inf)
        own_score = jnp.sum(
            queries.astype(F32) * key_new.astype(F32), axis=-1, keepdims=True
        ) * factor
        top = jnp.maximum(jnp.max(scores, axis=-1, keepdims=True), own_score)
        expo = jnp.exp(scores - top)
        own_expo = jnp.exp(own_score - top)
        inverse = 1.0 / (jnp.sum(expo, axis=-1, keepdims=True) + own_expo)
        weights = (expo * inverse).astype(BF16)
        own_weight = (own_expo * inverse).astype(BF16).astype(F32)
        mixed = dot(weights, vc[:, span]) + own_weight * value_new.astype(F32)
        for h in range(group):
            attended[:, (g * group + h) * HEAD:(g * group + h + 1) * HEAD] = mixed[
                h * docs:(h + 1) * docs
            ].astype(BF16)

    received(old_far)
    start(old_near[1:])

    def project_out(step, carry):
        output_copy(step).wait()
        block = output_block(step)
        span = pl.ds(pl.multiple_of(block * cols, cols), cols)
        part[block % 2, block // 2] = dot(attended[...], wo[:, span])
        return carry

    lax.fori_loop(0, mp_half, project_out, 0)
    part_near = remote(part.at[1 - core], part_in, part_a, 0, mp_slow * 2 + 1 - core, row)
    part_near.start()
    lax.fori_loop(mp_half, n_mp, project_out, 0)

    received([part_near])
    part_sum[...] = part[core] + part_in[...]
    part_apart = reduce_far(part_sum, part_far, part_b)
    start(part_apart)

    received(old_near)
    loads[2].wait()
    olds = old_all[...].reshape(anchors, cols)
    for right, base in ((sl, 0), (None, slab_rows)):
        product = dot(olds, olds if right is None else right[...], 1, 1)
        for j in range(n_mp):
            side[j % 2, j // 2, :, base:base + product.shape[1]] = product[
                j * share:(j + 1) * share
            ]
    side_near = remote(side.at[1 - core], side_in, side_a, 0, mp_slow * 2 + 1 - core, row)
    side_near.start()

    received(part_apart)
    state = hidden[:, mine].astype(F32) + part_sum[mp_slow]
    for off in range(1, mp_half):
        state = state + part_far[off - 1]
    square = jnp.sum(state * state, axis=-1, keepdims=True)
    sq_own[...] = jnp.broadcast_to(square, sq_own.shape)
    sq_copies = [
        remote(sq_own, sq_in.at[off - 1], sq_sem, off - 1, lax.rem(mp + off, n_mp), row)
        for off in range(1, n_mp)
    ]
    start(sq_copies)

    received([side_near])
    side_sum[...] = side[core] + side_in[...]
    side_apart = reduce_far(side_sum, side_far, side_b)
    start(side_apart)

    received(sq_copies)
    total = sq_own[...]
    for off in range(1, n_mp):
        total = total + sq_in[off - 1]
    scale = lax.rsqrt(total[:, :1] / width + 1e-06)
    new_all[row] = (state * scale * final_gain[:, mine]).astype(BF16)
    new_far = far_rows(new_all, new_f)
    start(new_far)
    new_near = near_rows(new_all, new_n)
    new_near[0].start()

    lanes = lax.broadcasted_iota(jnp.int32, (slab_rows, HEAD), 1)
    chosen = jnp.where(owners[...] == lanes, 1.0, 0.0)
    earlier = jnp.where(
        lax.broadcasted_iota(jnp.int32, (slab_rows, slab_rows), 1)
        < lax.broadcasted_iota(jnp.int32, (slab_rows, slab_rows), 0), 1.0, 0.0
    )
    slot = jnp.sum(
        dot(earlier.astype(BF16), chosen.astype(BF16)) * chosen, axis=-1, keepdims=True
    )
    target = owners[...].astype(F32) * cap + slot

    received(side_apart)
    whole = side_sum[mp_slow]
    for off in range(1, mp_half):
        whole = whole + side_far[off - 1]
    gram[mp] = whole[:, slab_rows:]
    gram_far = far_mp(gram, gram_f)
    start(gram_far)
    gram_near = near_mp(gram, gram_n)
    gram_near[0].start()
    body = whole[:, :slab_rows].astype(BF16)
    seats = lax.broadcasted_iota(jnp.int32, (slab_rows, cap), 1).astype(F32)
    for o in range(n_rows):
        put = jnp.where(target == seats + float(o * cap), 1.0, 0.0).astype(BF16)
        outgoing[o] = dot(body, put).astype(BF16)
    trips = []
    for off in range(1, n_rows):
        there = lax.rem(row + off, n_rows)
        trips.append(remote(outgoing.at[there], routed.at[mp, row], trip_sem, off - 1, mp, there))
    start(trips)
    routed[mp, row] = outgoing[row]

    received(new_far)
    start(new_near[1:])
    received(gram_far)
    start(gram_near[1:])

    received(trips)
    routed_far = far_mp(routed, routed_f)
    start(routed_far)
    routed_near = near_mp(routed, routed_n)
    routed_near[0].start()
    received(routed_far)
    start(routed_near[1:])

    received(gram_near)
    received(new_near)
    outs = [
        pltpu.make_async_copy(gram, gram_out, out_sem.at[0]),
        pltpu.make_async_copy(new_all, new_out, out_sem.at[1]),
    ]
    start(outs)
    received(routed_near)
    outs.append(pltpu.make_async_copy(routed, routed_out, out_sem.at[2]))
    outs[2].start()
    for copy in sent:
        copy.wait_send()
    for copy in outs:
        copy.wait()


def solve_kernel(ridge, targets, gram, routed, out):
    anchors = gram.shape[0]
    n_rows, cap = routed.shape[1], routed.shape[3]
    high = gram[...].astype(BF16)
    low = (gram[...] - high.astype(F32)).astype(BF16)

    def apply(values):
        top = values.astype(BF16)
        rest = (values - top.astype(F32)).astype(BF16)
        return dot(high, top) + (dot(high, rest) + dot(low, top))

    def total(values):
        return jnp.sum(values, axis=0, keepdims=True)

    start = targets[...]
    residual = start.astype(F32)
    direction = residual
    image_docs = dot(high, start) + dot(low, start)
    res_sq = total(residual * image_docs)
    coeffs = jnp.zeros_like(residual)
    for sweep in range(ITERS):
        curvature = total(image_docs * image_docs) + ridge * total(direction * image_docs)
        alpha = res_sq / curvature
        coeffs = coeffs + alpha * direction
        if sweep + 1 < ITERS:
            residual = residual - alpha * (image_docs + ridge * direction)
            spread = apply(residual)
            new_sq = total(residual * spread)
            ratio = new_sq / res_sq
            direction = residual + ratio * direction
            image_docs = spread + ratio * image_docs
            res_sq = new_sq
    top = coeffs.astype(BF16)
    rest = (coeffs - top.astype(F32)).astype(BF16)
    for b in range(n_rows):
        block = routed[:, b].reshape(anchors, cap)
        out[b * cap:(b + 1) * cap, :] = (dot(block, top, 0, 0) + dot(block, rest, 0, 0)).astype(BF16)


def local(
    hidden, attn_gain, w_query, w_key, w_value, w_output, query_gain, key_gain,
    key_cache, value_cache, lengths, final_gain, old_embed, slab, owners,
):
    n_rows = lax.axis_size("rows")
    n_mp = lax.axis_size("mp")
    docs, width = hidden.shape
    cols = width // n_mp
    anchors = n_rows * docs
    share = anchors // n_mp
    slab_rows = slab.shape[0]
    cap = 2 * slab_rows // n_rows
    kv_width = w_key.shape[1]
    q_width = w_query.shape[1]
    mp_half, rows_half = n_mp // 2, n_rows // 2
    key_cache = key_cache.reshape(-1, kv_width)
    value_cache = value_cache.reshape(-1, kv_width)
    side_width = slab_rows + anchors
    far_mp, far_rows = max(mp_half - 1, 1), max(rows_half - 1, 1)
    hbm = pl.BlockSpec(memory_space=pl.ANY)
    vmem = pl.BlockSpec(memory_space=pltpu.VMEM)
    dma = pltpu.SemaphoreType.DMA
    new_all, gram, routed = pl.pallas_call(
        functools.partial(encode_kernel, n_mp, n_rows),
        out_shape=(
            jax.ShapeDtypeStruct((n_rows, docs, cols), BF16),
            jax.ShapeDtypeStruct((n_mp, share, anchors), F32),
            jax.ShapeDtypeStruct((n_mp, n_rows, share, cap), BF16),
        ),
        in_specs=[
            vmem, vmem, hbm, hbm, hbm, hbm, vmem, vmem, hbm, hbm, vmem, vmem, vmem, hbm, vmem,
        ],
        out_specs=(hbm, hbm, hbm),
        scratch_shapes=[
            pltpu.VMEM((width, q_width), BF16),
            pltpu.VMEM((width, kv_width), BF16),
            pltpu.VMEM((width, kv_width), BF16),
            pltpu.VMEM((q_width, width), BF16),
            pltpu.VMEM(key_cache.shape, BF16),
            pltpu.VMEM(value_cache.shape, BF16),
            pltpu.VMEM(slab.shape, BF16),
            pltpu.VMEM((docs, width), BF16),
            pltpu.VMEM((docs, q_width), F32),
            pltpu.VMEM((docs, kv_width), F32),
            pltpu.VMEM((docs, kv_width), F32),
            pltpu.VMEM((docs, q_width), BF16),
            pltpu.VMEM((2, mp_half, docs, cols), F32),
            pltpu.VMEM((mp_half, docs, cols), F32),
            pltpu.VMEM((mp_half, docs, cols), F32),
            pltpu.VMEM((far_mp, docs, cols), F32),
            pltpu.VMEM((docs, 128), F32),
            pltpu.VMEM((n_mp - 1, docs, 128), F32),
            pltpu.VMEM((n_rows, docs, cols), BF16),
            pltpu.VMEM((n_rows, docs, cols), BF16),
            pltpu.VMEM((2, mp_half, share, side_width), F32),
            pltpu.VMEM((mp_half, share, side_width), F32),
            pltpu.VMEM((mp_half, share, side_width), F32),
            pltpu.VMEM((far_mp, share, side_width), F32),
            pltpu.VMEM((n_rows, share, cap), BF16),
            pltpu.VMEM((n_mp, n_rows, share, cap), BF16),
            pltpu.VMEM((n_mp, share, anchors), F32),
            dma((3,)), dma((3, CHUNKS)), dma((n_mp,)),
            dma((2, 1)), dma((2, far_mp)), dma((2, n_mp - 1)),
            dma((2, far_rows)), dma((2, rows_half)),
            dma((2, far_rows)), dma((2, rows_half)),
            dma((2, 1)), dma((2, far_mp)),
            dma((2, n_rows - 1)),
            dma((2, far_mp)), dma((2, mp_half)),
            dma((2, far_mp)), dma((2, mp_half)),
            dma((3,)),
        ],
        compiler_params=pltpu.CompilerParams(
            collective_id=0, has_side_effects=True, vmem_limit_bytes=56 * 2**20
        ),
        name="encode",
    )(
        hidden, attn_gain.reshape(1, -1), w_query, w_key, w_value, w_output,
        query_gain.reshape(1, -1), key_gain.reshape(1, -1), key_cache, value_cache,
        lengths.reshape(1, -1), final_gain.reshape(1, -1), old_embed, slab, owners,
    )
    tile = min(256, cols)
    return pl.pallas_call(
        functools.partial(solve_kernel, 0.125 * D),
        out_shape=jax.ShapeDtypeStruct((n_rows * cap, cols), BF16),
        grid=(cols // tile,),
        in_specs=[
            pl.BlockSpec((anchors, tile), lambda i: (0, i)),
            pl.BlockSpec((anchors, anchors), lambda i: (0, 0)),
            pl.BlockSpec((n_mp, n_rows, share, cap), lambda i: (0, 0, 0, 0)),
        ],
        out_specs=pl.BlockSpec((n_rows * cap, tile), lambda i: (0, i)),
        compiler_params=pltpu.CompilerParams(vmem_limit_bytes=48 * 2**20),
        name="solve",
    )(new_all.reshape(anchors, cols), gram.reshape(anchors, anchors), routed)


def solution(mesh):
    return jax.shard_map(
        local,
        mesh=mesh,
        in_specs=(
            P("rows", None),
            P(),
            P(None, "mp"),
            P(None, "mp"),
            P(None, "mp"),
            P("mp", None),
            P(),
            P(),
            P("rows", None, "mp"),
            P("rows", None, "mp"),
            P("rows"),
            P(),
            P("rows", None),
            P("rows", "mp"),
            P("rows", None),
        ),
        out_specs=P("rows", "mp"),
        check_vma=False,
    )
```

```python
import functools
import math

import jax
import jax.numpy as jnp
from jax import lax
from jax.experimental import pallas as pl
from jax.experimental.pallas import tpu as pltpu
from jax.sharding import PartitionSpec as P

D = 4096
HEADS = 32
KV_HEADS = 8
HEAD = 128
ITERS = 3
MESH = pl.DeviceIdType.MESH
F32 = jnp.float32
BF16 = jnp.bfloat16
CHUNKS = 8


def dot(left, right, left_dim=1, right_dim=0):
    return lax.dot_general(
        left, right, (((left_dim,), (right_dim,)), ((), ())), preferred_element_type=F32
    )


def solve(ridge, start, gram):
    high = gram.astype(BF16)
    low = (gram - high.astype(F32)).astype(BF16)

    def apply(values):
        top = values.astype(BF16)
        rest = (values - top.astype(F32)).astype(BF16)
        return dot(high, top) + (dot(high, rest) + dot(low, top))

    def total(values):
        return jnp.sum(values, axis=0, keepdims=True)

    residual = start
    direction = residual
    image_docs = apply(start)
    res_sq = total(residual * image_docs)
    coeffs = jnp.zeros_like(residual)
    for sweep in range(ITERS):
        curvature = total(image_docs * image_docs) + ridge * total(direction * image_docs)
        alpha = res_sq / curvature
        coeffs = coeffs + alpha * direction
        if sweep + 1 < ITERS:
            residual = residual - alpha * (image_docs + ridge * direction)
            spread = apply(residual)
            new_sq = total(residual * spread)
            ratio = new_sq / res_sq
            direction = residual + ratio * direction
            image_docs = spread + ratio * image_docs
            res_sq = new_sq
    return coeffs


def encode_kernel(
    n_mp, n_rows,
    hidden, attn_gain, w_query, w_key, w_value, w_output, query_gain, key_gain,
    key_cache, value_cache, lengths, final_gain, old_embed, slab, owners,
    out,
    wq, wk, wv, wo, kc, vc, sl, normed, q_acc, k_acc, v_acc, attended,
    part, part_in, part_sum, part_far, sq_own, sq_in, scale_all, new_all,
    old_all, side, side_in, side_sum, side_far, pair, pair_in, pair_sum, pair_far,
    outgoing, routed, gram, staged,
    load_sem, weight_sem, wo_sem,
    part_a, part_b, sq_sem, scale_sem, new_f, new_n, old_f, old_n,
    side_a, side_b, pair_a, pair_b,
    trip_sem, gram_f, gram_n, routed_f, routed_n, out_sem,
):
    mp = lax.axis_index("mp")
    row = lax.axis_index("rows")
    docs, width = hidden.shape
    cols = width // n_mp
    anchors = n_rows * docs
    share = anchors // n_mp
    slab_rows = slab.shape[0]
    cap = outgoing.shape[2]
    chunks, tile = new_all.shape[0], new_all.shape[3]
    kv_local = k_acc.shape[1] // HEAD
    group = HEADS // KV_HEADS
    ctx = key_cache.shape[0] // docs
    mp_half, rows_half = n_mp // 2, n_rows // 2
    mp_slow, core = mp // 2, mp % 2
    row_slow, row_fast = row // 2, row % 2

    def remote(src, dst, sems, spot, to_mp, to_row):
        spot = spot if isinstance(spot, tuple) else (spot,)
        return pltpu.make_async_remote_copy(
            src_ref=src, dst_ref=dst, send_sem=sems.at[(0, *spot)],
            recv_sem=sems.at[(1, *spot)],
            device_id={"mp": to_mp, "rows": to_row}, device_id_type=MESH,
        )

    def far_rows(buf, sems, *lead):
        return [
            remote(buf.at[(*lead, row)], buf.at[(*lead, row)], sems, (*lead, off - 1), mp,
                   ((row_slow + off) % rows_half) * 2 + row_fast)
            for off in range(1, rows_half)
        ]

    def near_rows(buf, sems, *lead):
        found = []
        for off in range(rows_half):
            block = ((row_slow + rows_half - off) % rows_half) * 2 + row_fast
            found.append(remote(buf.at[(*lead, block)], buf.at[(*lead, block)], sems,
                                (*lead, off), mp, row_slow * 2 + 1 - row_fast))
        return found

    def far_mp(buf, sems):
        return [
            remote(buf.at[mp], buf.at[mp], sems, off - 1,
                   ((mp_slow + off) % mp_half) * 2 + core, row)
            for off in range(1, mp_half)
        ]

    def near_mp(buf, sems):
        found = []
        for off in range(mp_half):
            block = ((mp_slow + mp_half - off) % mp_half) * 2 + core
            found.append(remote(buf.at[block], buf.at[block], sems, off,
                                mp_slow * 2 + 1 - core, row))
        return found

    def reduce_near(partial, landed, sems, *lead):
        return remote(partial.at[(*lead, 1 - core)], landed.at[lead] if lead else landed, sems,
                      (*lead, 0), mp_slow * 2 + 1 - core, row)

    def reduce_far(summed, landed, sems, *lead):
        found = []
        for off in range(1, mp_half):
            there = (mp_slow + off) % mp_half
            found.append(remote(summed.at[(*lead, there)], landed.at[(*lead, off - 1)], sems,
                                (*lead, off - 1), there * 2 + core, row))
        return found

    def start(copies):
        for copy in copies:
            copy.start()

    sent = []

    def received(copies):
        for copy in copies:
            copy.wait_recv()
            sent.append(copy)

    depth = width // CHUNKS

    def weight_copies(step):
        span = pl.ds(pl.multiple_of(step * depth, depth), depth)
        return [
            pltpu.make_async_copy(src.at[span, :], dst.at[span, :], weight_sem.at[i, step])
            for i, (src, dst) in enumerate(((w_query, wq), (w_key, wk), (w_value, wv)))
        ]

    def output_block(step):
        step = step % n_mp
        return 2 * (step % mp_half) + lax.rem(core + 1 + step // mp_half, 2)

    def output_span(step):
        base = output_block(step) * cols + step // n_mp * tile
        return pl.ds(pl.multiple_of(base, tile), tile)

    def output_copy(step):
        span = output_span(step)
        return pltpu.make_async_copy(w_output.at[:, span], wo.at[:, span], wo_sem.at[step])

    for step in range(CHUNKS):
        start(weight_copies(step))
    loads = [
        pltpu.make_async_copy(key_cache, kc, load_sem.at[0]),
        pltpu.make_async_copy(value_cache, vc, load_sem.at[1]),
        pltpu.make_async_copy(slab, sl, load_sem.at[2]),
    ]
    start(loads)
    for step in range(n_mp * chunks):
        output_copy(step).start()

    barrier = pltpu.get_barrier_semaphore()
    for off in range(1, n_rows):
        pl.semaphore_signal(barrier, inc=1, device_id={"mp": mp, "rows": lax.rem(row + off, n_rows)},
                            device_id_type=MESH)
    for off in range(1, n_mp):
        pl.semaphore_signal(barrier, inc=1, device_id={"mp": lax.rem(mp + off, n_mp), "rows": row},
                            device_id_type=MESH)
    mine = pl.ds(pl.multiple_of(mp * cols, cols), cols)
    old_all[row] = old_embed[:, mine]
    pl.semaphore_wait(barrier, n_rows + n_mp - 2)

    old_far = far_rows(old_all, old_f)
    start(old_far)
    old_near = near_rows(old_all, old_n)
    old_near[0].start()

    hidden32 = hidden[...].astype(F32)
    normed[...] = (
        hidden32 * lax.rsqrt(jnp.mean(hidden32 * hidden32, axis=-1, keepdims=True) + 1e-06)
        * attn_gain[...]
    ).astype(BF16)

    q_acc[...] = jnp.zeros_like(q_acc)
    k_acc[...] = jnp.zeros_like(k_acc)
    v_acc[...] = jnp.zeros_like(v_acc)

    def project(step, carry):
        span = pl.ds(pl.multiple_of(step * depth, depth), depth)
        for copy in weight_copies(step):
            copy.wait()
        piece = normed[:, span]
        q_acc[...] += dot(piece, wq[span, :])
        k_acc[...] += dot(piece, wk[span, :])
        v_acc[...] += dot(piece, wv[span, :])
        return carry

    lax.fori_loop(0, CHUNKS, project, 0)

    received(old_far)
    start(old_near[1:])

    tall = group * docs
    spot = lax.broadcasted_iota(jnp.int32, (tall, docs), 0) % docs
    named = lax.broadcasted_iota(jnp.int32, (tall, docs), 1)
    length = jnp.sum(
        jnp.where(spot == named, lengths[...].astype(F32), 0.0), axis=-1, keepdims=True
    )
    lane = lax.broadcasted_iota(jnp.int32, (docs, HEAD), 1)
    half = HEAD // 2
    frequency = jnp.exp(
        -(2.0 * (lane % half).astype(F32) / HEAD) * math.log(1000000.0)
    )
    angle = length[:docs] * frequency
    cosine = jnp.cos(angle)
    sine = jnp.sin(angle) * jnp.where(lane < half, -1.0, 1.0)

    def turned(values, gain):
        scale = lax.rsqrt(jnp.mean(values * values, axis=-1, keepdims=True) + 1e-06)
        values = values * scale * gain
        return (values * cosine + pltpu.roll(values, half, 1) * sine).astype(BF16)

    loads[0].wait()
    loads[1].wait()
    place_row = lax.broadcasted_iota(jnp.int32, (tall, docs * ctx), 0) % docs * ctx
    place_lane = lax.broadcasted_iota(jnp.int32, (tall, docs * ctx), 1)
    valid = (place_lane >= place_row) & (place_lane < place_row + length.astype(jnp.int32))
    for g in range(kv_local):
        span = slice(g * HEAD, (g + 1) * HEAD)
        queries = jnp.concatenate(
            [
                turned(q_acc[:, (g * group + h) * HEAD:(g * group + h + 1) * HEAD], query_gain[...])
                for h in range(group)
            ],
            axis=0,
        )
        key_new = jnp.concatenate([turned(k_acc[:, span], key_gain[...])] * group, axis=0)
        value_new = jnp.concatenate([v_acc[:, span].astype(BF16)] * group, axis=0)
        factor = 1.0 / math.sqrt(HEAD)
        scores = jnp.where(valid, dot(queries, kc[:, span], 1, 1) * factor, -jnp.inf)
        own_score = jnp.sum(
            queries.astype(F32) * key_new.astype(F32), axis=-1, keepdims=True
        ) * factor
        top = jnp.maximum(jnp.max(scores, axis=-1, keepdims=True), own_score)
        expo = jnp.exp(scores - top)
        own_expo = jnp.exp(own_score - top)
        inverse = 1.0 / (jnp.sum(expo, axis=-1, keepdims=True) + own_expo)
        weights = (expo * inverse).astype(BF16)
        own_weight = (own_expo * inverse).astype(BF16).astype(F32)
        mixed = dot(weights, vc[:, span]) + own_weight * value_new.astype(F32)
        for h in range(group):
            attended[:, (g * group + h) * HEAD:(g * group + h + 1) * HEAD] = mixed[
                h * docs:(h + 1) * docs
            ].astype(BF16)

    def project_out(chunk, first):
        for step in range(first, first + mp_half):
            step = chunk * n_mp + step
            output_copy(step).wait()
            block = output_block(step)
            part[chunk, block % 2, block // 2] = dot(attended[...], wo[:, output_span(step)])

    part_near = [reduce_near(part, part_in, part_a, c) for c in range(chunks)]
    part_apart = [reduce_far(part_sum, part_far, part_b, c) for c in range(chunks)]

    def add_near(c):
        received([part_near[c]])
        part_sum[c] = part[c, core] + part_in[c]
        start(part_apart[c])

    for c in range(chunks):
        project_out(c, 0)
        part_near[c].start()
        project_out(c, mp_half)
        if c:
            add_near(c - 1)

    received(old_near)
    loads[2].wait()
    olds = old_all[...].reshape(anchors, cols)
    product = dot(olds, sl[...], 1, 1)
    for j in range(n_mp):
        side[j % 2, j // 2] = product[j * share:(j + 1) * share]
    side_near = reduce_near(side, side_in, side_a)
    side_near.start()
    add_near(chunks - 1)
    product = dot(olds, olds, 1, 1)
    for j in range(n_mp):
        pair[j % 2, j // 2] = product[j * share:(j + 1) * share]
    pair_near = reduce_near(pair, pair_in, pair_a)
    pair_near.start()

    new_far = [far_rows(new_all, new_f, c) for c in range(chunks)]
    new_near = [near_rows(new_all, new_n, c) for c in range(chunks)]
    square = jnp.zeros((docs, 1), F32)
    for c in range(chunks):
        received(part_apart[c])
        span = pl.ds(pl.multiple_of(mp * cols + c * tile, tile), tile)
        state = hidden[:, span].astype(F32) + part_sum[c, mp_slow]
        for off in range(1, mp_half):
            state = state + part_far[c, off - 1]
        new_all[c, row] = (state * final_gain[:, span]).astype(BF16)
        start(new_far[c])
        new_near[c][0].start()
        square = square + jnp.sum(state * state, axis=-1, keepdims=True)
    sq_own[...] = jnp.broadcast_to(square, sq_own.shape)
    sq_copies = [
        remote(sq_own, sq_in.at[off - 1], sq_sem, off - 1, lax.rem(mp + off, n_mp), row)
        for off in range(1, n_mp)
    ]
    start(sq_copies)

    received([side_near])
    side_sum[...] = side[core] + side_in[...]
    side_apart = reduce_far(side_sum, side_far, side_b)
    start(side_apart)
    received([pair_near])
    pair_sum[...] = pair[core] + pair_in[...]
    pair_apart = reduce_far(pair_sum, pair_far, pair_b)
    start(pair_apart)

    owner = owners[...]
    chosen = jnp.where(
        owner == lax.broadcasted_iota(jnp.int32, (n_rows, slab_rows), 0), 1.0, 0.0
    )
    earlier = jnp.where(
        lax.broadcasted_iota(jnp.int32, (slab_rows, slab_rows), 0)
        < lax.broadcasted_iota(jnp.int32, (slab_rows, slab_rows), 1), 1.0, 0.0
    )
    slot = jnp.sum(
        dot(chosen.astype(BF16), earlier.astype(BF16)) * chosen, axis=0, keepdims=True
    )
    target = owner.astype(F32) * cap + slot

    received(sq_copies)
    total = sq_own[...]
    for off in range(1, n_mp):
        total = total + sq_in[off - 1]
    scale_all[row] = lax.rsqrt(total / width + 1e-06)
    scale_copies = [
        remote(scale_all.at[row], scale_all.at[row], scale_sem, off - 1, mp,
               lax.rem(row + off, n_rows))
        for off in range(1, n_rows)
    ]
    start(scale_copies)

    def forward(c):
        received(new_far[c])
        start(new_near[c][1:])

    for c in range(chunks // 2):
        forward(c)

    received(side_apart)
    whole = side_sum[mp_slow]
    for off in range(1, mp_half):
        whole = whole + side_far[off - 1]
    body = whole.astype(BF16)
    seats = lax.broadcasted_iota(jnp.int32, (cap, slab_rows), 0).astype(F32)
    for o in range(n_rows):
        put = jnp.where(target == seats + float(o * cap), 1.0, 0.0).astype(BF16)
        outgoing[o] = dot(body, put, 1, 1).astype(BF16)
    trips = []
    for off in range(1, n_rows):
        there = lax.rem(row + off, n_rows)
        trips.append(remote(outgoing.at[there], routed.at[mp, row], trip_sem, off - 1, mp, there))
    start(trips)
    routed[mp, row] = outgoing[row]

    received(pair_apart)
    whole = pair_sum[mp_slow]
    for off in range(1, mp_half):
        whole = whole + pair_far[off - 1]
    gram[mp] = whole
    gram_far = far_mp(gram, gram_f)
    start(gram_far)
    gram_near = near_mp(gram, gram_n)
    gram_near[0].start()

    for c in range(chunks // 2, chunks):
        forward(c)

    received(trips)
    routed_far = far_mp(routed, routed_f)
    start(routed_far)
    routed_near = near_mp(routed, routed_n)
    routed_near[0].start()
    received(gram_far)
    start(gram_near[1:])
    received(routed_far)
    start(routed_near[1:])

    received(gram_near)
    received(scale_copies)
    scale = scale_all[...].reshape(anchors, HEAD)[:, :1]
    outs = []
    for c in range(chunks):
        received(new_near[c])
        targets = new_all[c].reshape(anchors, tile).astype(F32) * scale
        coeffs = solve(0.125 * D, targets, gram[...].reshape(anchors, anchors))
        top = coeffs.astype(BF16)
        rest = (coeffs - top.astype(F32)).astype(BF16)
        if c == 0:
            received(routed_near)
        for b in range(n_rows):
            block = routed[:, b].reshape(anchors, cap)
            staged[c, b * cap:(b + 1) * cap] = (
                dot(block, top, 0, 0) + dot(block, rest, 0, 0)
            ).astype(BF16)
        outs.append(
            pltpu.make_async_copy(
                staged.at[c], out.at[:, c * tile:(c + 1) * tile], out_sem.at[c]
            )
        )
        outs[c].start()
    for copy in sent:
        copy.wait_send()
    for copy in outs:
        copy.wait()


def local(
    hidden, attn_gain, w_query, w_key, w_value, w_output, query_gain, key_gain,
    key_cache, value_cache, lengths, final_gain, old_embed, slab, owners,
):
    n_rows = lax.axis_size("rows")
    n_mp = lax.axis_size("mp")
    docs, width = hidden.shape
    cols = width // n_mp
    anchors = n_rows * docs
    share = anchors // n_mp
    slab_rows = slab.shape[0]
    cap = 2 * slab_rows // n_rows
    kv_width = w_key.shape[1]
    q_width = w_query.shape[1]
    mp_half, rows_half = n_mp // 2, n_rows // 2
    key_cache = key_cache.reshape(-1, kv_width)
    value_cache = value_cache.reshape(-1, kv_width)
    tile = min(256, cols)
    chunks = cols // tile
    far_mp, far_rows = max(mp_half - 1, 1), max(rows_half - 1, 1)
    hbm = pl.BlockSpec(memory_space=pl.ANY)
    vmem = pl.BlockSpec(memory_space=pltpu.VMEM)
    dma = pltpu.SemaphoreType.DMA
    return pl.pallas_call(
        functools.partial(encode_kernel, n_mp, n_rows),
        out_shape=jax.ShapeDtypeStruct((n_rows * cap, cols), BF16),
        in_specs=[
            vmem, vmem, hbm, hbm, hbm, hbm, vmem, vmem, hbm, hbm, vmem, vmem, vmem, hbm, vmem,
        ],
        out_specs=hbm,
        scratch_shapes=[
            pltpu.VMEM((width, q_width), BF16),
            pltpu.VMEM((width, kv_width), BF16),
            pltpu.VMEM((width, kv_width), BF16),
            pltpu.VMEM((q_width, width), BF16),
            pltpu.VMEM(key_cache.shape, BF16),
            pltpu.VMEM(value_cache.shape, BF16),
            pltpu.VMEM(slab.shape, BF16),
            pltpu.VMEM((docs, width), BF16),
            pltpu.VMEM((docs, q_width), F32),
            pltpu.VMEM((docs, kv_width), F32),
            pltpu.VMEM((docs, kv_width), F32),
            pltpu.VMEM((docs, q_width), BF16),
            pltpu.VMEM((chunks, 2, mp_half, docs, tile), F32),
            pltpu.VMEM((chunks, mp_half, docs, tile), F32),
            pltpu.VMEM((chunks, mp_half, docs, tile), F32),
            pltpu.VMEM((chunks, far_mp, docs, tile), F32),
            pltpu.VMEM((docs, 128), F32),
            pltpu.VMEM((n_mp - 1, docs, 128), F32),
            pltpu.VMEM((n_rows, docs, 128), F32),
            pltpu.VMEM((chunks, n_rows, docs, tile), BF16),
            pltpu.VMEM((n_rows, docs, cols), BF16),
            pltpu.VMEM((2, mp_half, share, slab_rows), F32),
            pltpu.VMEM((mp_half, share, slab_rows), F32),
            pltpu.VMEM((mp_half, share, slab_rows), F32),
            pltpu.VMEM((far_mp, share, slab_rows), F32),
            pltpu.VMEM((2, mp_half, share, anchors), F32),
            pltpu.VMEM((mp_half, share, anchors), F32),
            pltpu.VMEM((mp_half, share, anchors), F32),
            pltpu.VMEM((far_mp, share, anchors), F32),
            pltpu.VMEM((n_rows, share, cap), BF16),
            pltpu.VMEM((n_mp, n_rows, share, cap), BF16),
            pltpu.VMEM((n_mp, share, anchors), F32),
            pltpu.VMEM((chunks, n_rows * cap, tile), BF16),
            dma((3,)), dma((3, CHUNKS)), dma((n_mp * chunks,)),
            dma((2, chunks, 1)), dma((2, chunks, far_mp)), dma((2, n_mp - 1)),
            dma((2, n_rows - 1)),
            dma((2, chunks, far_rows)), dma((2, chunks, rows_half)),
            dma((2, far_rows)), dma((2, rows_half)),
            dma((2, 1)), dma((2, far_mp)),
            dma((2, 1)), dma((2, far_mp)),
            dma((2, n_rows - 1)),
            dma((2, far_mp)), dma((2, mp_half)),
            dma((2, far_mp)), dma((2, mp_half)),
            dma((chunks,)),
        ],
        compiler_params=pltpu.CompilerParams(
            collective_id=0, has_side_effects=True, vmem_limit_bytes=56 * 2**20
        ),
        name="encode",
    )(
        hidden, attn_gain.reshape(1, -1), w_query, w_key, w_value, w_output,
        query_gain.reshape(1, -1), key_gain.reshape(1, -1), key_cache, value_cache,
        lengths.reshape(1, -1), final_gain.reshape(1, -1), old_embed, slab, owners.reshape(1, -1),
    )

def solution(mesh):
    return jax.shard_map(
        local,
        mesh=mesh,
        in_specs=(
            P("rows", None),
            P(),
            P(None, "mp"),
            P(None, "mp"),
            P(None, "mp"),
            P("mp", None),
            P(),
            P(),
            P("rows", None, "mp"),
            P("rows", None, "mp"),
            P("rows"),
            P(),
            P("rows", None),
            P("rows", "mp"),
            P("rows", None),
        ),
        out_specs=P("rows", "mp"),
        check_vma=False,
    )
```

```python
import functools
import math

import jax
import jax.numpy as jnp
from jax import lax
from jax.experimental import pallas as pl
from jax.experimental.pallas import tpu as pltpu
from jax.sharding import PartitionSpec as P

D = 4096
HEADS = 32
KV_HEADS = 8
HEAD = 128
ITERS = 3
MESH = pl.DeviceIdType.MESH
F32 = jnp.float32
BF16 = jnp.bfloat16
CHUNKS = 8


def dot(left, right, left_dim=1, right_dim=0):
    return lax.dot_general(
        left, right, (((left_dim,), (right_dim,)), ((), ())), preferred_element_type=F32
    )


def solve(ridge, start, gram):
    high = gram.astype(BF16)
    low = (gram - high.astype(F32)).astype(BF16)

    def apply(values):
        top = values.astype(BF16)
        rest = (values - top.astype(F32)).astype(BF16)
        return dot(high, top) + (dot(high, rest) + dot(low, top))

    def total(values):
        return jnp.sum(values, axis=0, keepdims=True)

    residual = start
    direction = residual
    image_docs = apply(start)
    res_sq = total(residual * image_docs)
    coeffs = jnp.zeros_like(residual)
    for sweep in range(ITERS):
        curvature = total(image_docs * image_docs) + ridge * total(direction * image_docs)
        alpha = res_sq / curvature
        coeffs = coeffs + alpha * direction
        if sweep + 1 < ITERS:
            residual = residual - alpha * (image_docs + ridge * direction)
            spread = apply(residual)
            new_sq = total(residual * spread)
            ratio = new_sq / res_sq
            direction = residual + ratio * direction
            image_docs = spread + ratio * image_docs
            res_sq = new_sq
    return coeffs


def encode_kernel(
    n_mp, n_rows,
    hidden_in, attn_gain_in, w_query, w_key, w_value, w_output, query_gain_in, key_gain_in,
    key_cache, value_cache, lengths_in, final_gain_in, old_embed, slab, owners_in,
    out,
    hidden, attn_gain, query_gain, key_gain, lengths, final_gain, owners,
    wq, wk, wv, wo, kc, vc, sl, normed, q_acc, k_acc, v_acc, attended,
    part, part_in, part_sum, part_far, sq_own, sq_in, scale_all, new_all,
    old_all, side, side_in, side_sum, side_far, pair, pair_in, pair_sum, pair_far,
    outgoing, routed, gram, spread_length, spread_scale, mapped, rows_t, puts, staged,
    load_sem, weight_sem, wo_sem,
    part_a, part_b, sq_sem, scale_sem, new_f, new_n, old_f, old_n,
    side_a, side_b, pair_a, pair_b,
    trip_sem, gram_f, gram_n, routed_f, routed_n, out_sem,
):
    mp = lax.axis_index("mp")
    row = lax.axis_index("rows")
    docs, width = hidden.shape
    cols = width // n_mp
    anchors = n_rows * docs
    share = anchors // n_mp
    slab_rows = slab.shape[0]
    cap = outgoing.shape[2]
    chunks, tile = new_all.shape[0], new_all.shape[3]
    kv_local = k_acc.shape[1] // HEAD
    group = HEADS // KV_HEADS
    ctx = key_cache.shape[0] // docs
    mp_half, rows_half = n_mp // 2, n_rows // 2
    mp_slow, core = mp // 2, mp % 2
    row_slow, row_fast = row // 2, row % 2

    def remote(src, dst, sems, spot, to_mp, to_row):
        spot = spot if isinstance(spot, tuple) else (spot,)
        return pltpu.make_async_remote_copy(
            src_ref=src, dst_ref=dst, send_sem=sems.at[(0, *spot)],
            recv_sem=sems.at[(1, *spot)],
            device_id={"mp": to_mp, "rows": to_row}, device_id_type=MESH,
        )

    def far_rows(buf, sems, *lead):
        return [
            remote(buf.at[(*lead, row)], buf.at[(*lead, row)], sems, (*lead, off - 1), mp,
                   ((row_slow + off) % rows_half) * 2 + row_fast)
            for off in range(1, rows_half)
        ]

    def near_rows(buf, sems, *lead):
        found = []
        for off in range(rows_half):
            block = ((row_slow + rows_half - off) % rows_half) * 2 + row_fast
            found.append(remote(buf.at[(*lead, block)], buf.at[(*lead, block)], sems,
                                (*lead, off), mp, row_slow * 2 + 1 - row_fast))
        return found

    def far_mp(buf, sems):
        return [
            remote(buf.at[mp], buf.at[mp], sems, off - 1,
                   ((mp_slow + off) % mp_half) * 2 + core, row)
            for off in range(1, mp_half)
        ]

    def near_mp(buf, sems):
        found = []
        for off in range(mp_half):
            block = ((mp_slow + mp_half - off) % mp_half) * 2 + core
            found.append(remote(buf.at[block], buf.at[block], sems, off,
                                mp_slow * 2 + 1 - core, row))
        return found

    def reduce_near(partial, landed, sems, *lead):
        return remote(partial.at[(*lead, 1 - core)], landed.at[lead] if lead else landed, sems,
                      (*lead, 0), mp_slow * 2 + 1 - core, row)

    def reduce_far(summed, landed, sems, *lead):
        found = []
        for off in range(1, mp_half):
            there = (mp_slow + off) % mp_half
            found.append(remote(summed.at[(*lead, there)], landed.at[(*lead, off - 1)], sems,
                                (*lead, off - 1), there * 2 + core, row))
        return found

    def start(copies):
        for copy in copies:
            copy.start()

    sent = []

    def received(copies):
        for copy in copies:
            copy.wait_recv()
            sent.append(copy)

    depth = width // CHUNKS

    def weight_copies(step):
        span = pl.ds(pl.multiple_of(step * depth, depth), depth)
        return [
            pltpu.make_async_copy(src.at[span, :], dst.at[span, :], weight_sem.at[i, step])
            for i, (src, dst) in enumerate(((w_query, wq), (w_key, wk), (w_value, wv)))
        ]

    def output_block(step):
        step = step % n_mp
        return 2 * (step % mp_half) + lax.rem(core + 1 + step // mp_half, 2)

    def output_span(step):
        base = output_block(step) * cols + step // n_mp * tile
        return pl.ds(pl.multiple_of(base, tile), tile)

    def output_copy(step):
        span = output_span(step)
        return pltpu.make_async_copy(w_output.at[:, span], wo.at[:, span], wo_sem.at[step])

    barrier = pltpu.get_barrier_semaphore()
    for off in range(1, n_rows):
        pl.semaphore_signal(barrier, inc=1, device_id={"mp": mp, "rows": lax.rem(row + off, n_rows)},
                            device_id_type=MESH)
    for off in range(1, n_mp):
        pl.semaphore_signal(barrier, inc=1, device_id={"mp": lax.rem(mp + off, n_mp), "rows": row},
                            device_id_type=MESH)
    mine = pl.ds(pl.multiple_of(mp * cols, cols), cols)
    loads = [
        pltpu.make_async_copy(src, dst, load_sem.at[i])
        for i, (src, dst) in enumerate((
            (key_cache, kc), (value_cache, vc), (slab, sl),
            (hidden_in, hidden), (attn_gain_in, attn_gain),
            (old_embed.at[:, mine], old_all.at[row]), (owners_in, owners),
            (lengths_in, lengths), (query_gain_in, query_gain), (key_gain_in, key_gain),
            (final_gain_in, final_gain),
        ))
    ]
    start(loads[3:])
    for step in range(CHUNKS):
        start(weight_copies(step))
    start(loads[:3])
    for step in range(n_mp * chunks):
        output_copy(step).start()

    loads[3].wait()
    loads[4].wait()
    hidden32 = hidden[...].astype(F32)
    normed[...] = (
        hidden32 * lax.rsqrt(jnp.mean(hidden32 * hidden32, axis=-1, keepdims=True) + 1e-06)
        * attn_gain[...]
    ).astype(BF16)
    for copy in loads[5:]:
        copy.wait()
    pl.semaphore_wait(barrier, n_rows + n_mp - 2)

    old_far = far_rows(old_all, old_f)
    start(old_far)
    old_near = near_rows(old_all, old_n)
    old_near[0].start()

    q_acc[...] = jnp.zeros_like(q_acc)
    k_acc[...] = jnp.zeros_like(k_acc)
    v_acc[...] = jnp.zeros_like(v_acc)

    owner = owners[...]
    chosen = jnp.where(
        owner == lax.broadcasted_iota(jnp.int32, (n_rows, slab_rows), 0), 1.0, 0.0
    )
    earlier = jnp.where(
        lax.broadcasted_iota(jnp.int32, (slab_rows, slab_rows), 0)
        < lax.broadcasted_iota(jnp.int32, (slab_rows, slab_rows), 1), 1.0, 0.0
    )
    slot = jnp.sum(
        dot(chosen.astype(BF16), earlier.astype(BF16)) * chosen, axis=0, keepdims=True
    )
    target = owner.astype(F32) * cap + slot
    seats = lax.broadcasted_iota(jnp.int32, (cap, slab_rows), 0).astype(F32)

    def put(o, carry):
        base = (o * cap).astype(F32)
        puts[pl.ds(pl.multiple_of(o * cap, cap), cap)] = jnp.where(
            target - base == seats, 1.0, 0.0
        ).astype(BF16)
        return carry

    lax.fori_loop(0, n_rows, put, 0)

    def project(step, carry):
        span = pl.ds(pl.multiple_of(step * depth, depth), depth)
        for copy in weight_copies(step):
            copy.wait()
        piece = normed[:, span]
        q_acc[...] += dot(piece, wq[span, :])
        k_acc[...] += dot(piece, wk[span, :])
        v_acc[...] += dot(piece, wv[span, :])
        return carry

    done = CHUNKS // 2
    lax.fori_loop(0, done, project, 0)
    for off in range(1, rows_half):
        lax.fori_loop(done, max(done, CHUNKS * (rows_half + off) // (2 * rows_half)), project, 0)
        done = max(done, CHUNKS * (rows_half + off) // (2 * rows_half))
        received(old_far[off - 1:off])
        old_near[off].start()
    lax.fori_loop(done, CHUNKS, project, 0)

    spot = lax.broadcasted_iota(jnp.int32, (docs, docs), 0)
    named = lax.broadcasted_iota(jnp.int32, (docs, docs), 1)
    length = jnp.sum(
        jnp.where(spot == named, lengths[...].astype(F32), 0.0), axis=-1, keepdims=True
    )
    lane = lax.broadcasted_iota(jnp.int32, (docs, HEAD), 1)
    half = HEAD // 2
    frequency = jnp.exp(
        -(2.0 * (lane % half).astype(F32) / HEAD) * math.log(1000000.0)
    )
    angle = length * frequency
    cosine = jnp.cos(angle)
    sine = jnp.sin(angle) * jnp.where(lane < half, -1.0, 1.0)

    def turned(values, gain):
        scale = lax.rsqrt(jnp.mean(values * values, axis=-1, keepdims=True) + 1e-06)
        values = values * scale * gain
        return values * cosine + pltpu.roll(values, half, 1) * sine

    loads[0].wait()
    loads[1].wait()
    few = min(8, docs)
    tall, wide = group * few, few * ctx
    place_row = lax.broadcasted_iota(jnp.int32, (tall, wide), 0) % few * ctx
    place_lane = lax.broadcasted_iota(jnp.int32, (tall, wide), 1)
    factor = 1.0 / math.sqrt(HEAD)
    spread_length[...] = jnp.broadcast_to(length, spread_length.shape)

    def turn_query(h, carry):
        span = pl.ds(pl.multiple_of(h * HEAD, HEAD), HEAD)
        q_acc[:, span] = turned(q_acc[:, span], query_gain[...])
        return carry

    lax.fori_loop(0, kv_local * group, turn_query, 0)
    for g in range(kv_local):
        span = slice(g * HEAD, (g + 1) * HEAD)
        k_acc[:, span] = turned(k_acc[:, span], key_gain[...]).astype(BF16).astype(F32)
    v_acc[...] = v_acc[...].astype(BF16).astype(F32)

    def attend(block, carry):
        some = pl.ds(pl.multiple_of(block * few, few), few)
        held = pl.ds(pl.multiple_of(block * few * ctx, few * ctx), few * ctx)
        long = jnp.concatenate([spread_length[some, :1]] * group, axis=0).astype(jnp.int32)
        valid = (place_lane >= place_row) & (place_lane < place_row + long)
        for g in range(kv_local):
            span = slice(g * HEAD, (g + 1) * HEAD)
            heads = [
                slice((g * group + h) * HEAD, (g * group + h + 1) * HEAD) for h in range(group)
            ]
            ask = jnp.concatenate([q_acc[some, head] for head in heads], axis=0).astype(BF16)
            scores = jnp.where(valid, dot(ask, kc[held, span], 1, 1) * factor, -jnp.inf)
            own_score = jnp.sum(
                ask.astype(F32) * jnp.concatenate([k_acc[some, span]] * group, axis=0),
                axis=-1, keepdims=True,
            ) * factor
            top = jnp.maximum(jnp.max(scores, axis=-1, keepdims=True), own_score)
            expo = jnp.exp(scores - top)
            own_expo = jnp.exp(own_score - top)
            inverse = 1.0 / (jnp.sum(expo, axis=-1, keepdims=True) + own_expo)
            weights = (expo * inverse).astype(BF16)
            own_weight = (own_expo * inverse).astype(BF16).astype(F32)
            mixed = dot(weights, vc[held, span]) + own_weight * jnp.concatenate(
                [v_acc[some, span]] * group, axis=0
            )
            for h, head in enumerate(heads):
                q_acc[some, head] = mixed[h * few:(h + 1) * few]
        return carry

    lax.fori_loop(0, docs // few, attend, 0)
    attended[...] = q_acc[...].astype(BF16)

    def project_out(step, carry):
        output_copy(step).wait()
        block = output_block(step)
        part[step // n_mp, block % 2, block // 2] = dot(attended[...], wo[:, output_span(step)])
        return carry

    part_near = [reduce_near(part, part_in, part_a, c) for c in range(chunks)]
    part_apart = [reduce_far(part_sum, part_far, part_b, c) for c in range(chunks)]
    width_step = min(256, anchors, slab_rows)

    def multiply(into, right):
        def piece(step, carry):
            span = pl.ds(pl.multiple_of(step * width_step, width_step), width_step)
            product = dot(old_all[...].reshape(anchors, cols), right(span), 1, 1)
            for j in range(n_mp):
                into[j % 2, j // 2, :, span] = product[j * share:(j + 1) * share]
            return carry

        lax.fori_loop(0, into.shape[3] // width_step, piece, 0)

    def add_near(c):
        received([part_near[c]])
        part_sum[c] = part[c, core] + part_in[c]
        start(part_apart[c])

    side_near = reduce_near(side, side_in, side_a)
    side_apart = reduce_far(side_sum, side_far, side_b)
    pair_near = reduce_near(pair, pair_in, pair_a)
    pair_apart = reduce_far(pair_sum, pair_far, pair_b)
    for c in range(chunks):
        lax.fori_loop(c * n_mp, c * n_mp + mp_half, project_out, 0)
        part_near[c].start()
        lax.fori_loop(c * n_mp + mp_half, (c + 1) * n_mp, project_out, 0)
        if c == max(chunks // 2 - 1, 0):
            received(old_near)
            loads[2].wait()
            multiply(side, lambda span: sl[span])
            side_near.start()
        if c:
            add_near(c - 1)
    add_near(chunks - 1)
    received([side_near])
    side_sum[...] = side[core] + side_in[...]
    start(side_apart)
    docs_step = width_step // docs
    multiply(
        pair,
        lambda span: old_all[pl.ds(span.start // docs, docs_step)].reshape(width_step, cols),
    )
    pair_near.start()

    new_far = [far_rows(new_all, new_f, c) for c in range(chunks)]
    new_near = [near_rows(new_all, new_n, c) for c in range(chunks)]
    square = jnp.zeros((docs, 1), F32)
    for c in range(chunks):
        received(part_apart[c])
        span = pl.ds(pl.multiple_of(mp * cols + c * tile, tile), tile)
        state = hidden[:, span].astype(F32) + part_sum[c, mp_slow]
        for off in range(1, mp_half):
            state = state + part_far[c, off - 1]
        new_all[c, row] = (state * final_gain[:, span]).astype(BF16)
        start(new_far[c])
        new_near[c][0].start()
        square = square + jnp.sum(state * state, axis=-1, keepdims=True)
    sq_own[...] = jnp.broadcast_to(square, sq_own.shape)
    sq_copies = [
        remote(sq_own, sq_in.at[off - 1], sq_sem, off - 1, lax.rem(mp + off, n_mp), row)
        for off in range(1, n_mp)
    ]
    start(sq_copies)

    received(side_apart)
    whole = side_sum[mp_slow]
    for off in range(1, mp_half):
        whole = whole + side_far[off - 1]
    body = whole.astype(BF16)

    def place(o, carry):
        span = pl.ds(pl.multiple_of(o * cap, cap), cap)
        outgoing[o] = dot(body, puts[span], 1, 1).astype(BF16)
        return carry

    lax.fori_loop(0, n_rows, place, 0)
    trips = []
    for off in range(1, n_rows):
        there = lax.rem(row + off, n_rows)
        trips.append(remote(outgoing.at[there], routed.at[mp, row], trip_sem, off - 1, mp, there))
    start(trips)
    routed[mp, row] = outgoing[row]

    received(sq_copies)
    total = sq_own[...]
    for off in range(1, n_mp):
        total = total + sq_in[off - 1]
    scale_all[row] = lax.rsqrt(total / width + 1e-06)
    scale_copies = [
        remote(scale_all.at[row], scale_all.at[row], scale_sem, off - 1, mp,
               lax.rem(row + off, n_rows))
        for off in range(1, n_rows)
    ]
    start(scale_copies)

    received([pair_near])
    pair_sum[...] = pair[core] + pair_in[...]
    start(pair_apart)

    def forward(c):
        received(new_far[c])
        start(new_near[c][1:])

    for c in range(chunks // 2):
        forward(c)
    received(trips)
    routed_far = far_mp(routed, routed_f)
    start(routed_far)
    routed_near = near_mp(routed, routed_n)
    routed_near[0].start()
    received(pair_apart)
    whole = pair_sum[mp_slow]
    for off in range(1, mp_half):
        whole = whole + pair_far[off - 1]
    gram[mp] = whole
    gram_far = far_mp(gram, gram_f)
    start(gram_far)
    gram_near = near_mp(gram, gram_n)
    gram_near[0].start()

    for c in range(chunks // 2, chunks):
        forward(c)
    received(routed_far)
    start(routed_near[1:])
    received(gram_far)
    start(gram_near[1:])

    received(gram_near)
    received(scale_copies)
    scale = scale_all[...].reshape(anchors, HEAD)[:, :1]
    spread_scale[...] = jnp.broadcast_to(scale, spread_scale.shape)
    row_step = min(256, n_rows * cap)

    def turn_rows(b, carry):
        span = pl.ds(pl.multiple_of(b * cap, cap), cap)
        rows_t[span] = routed[:, b].reshape(anchors, cap).T
        return carry

    def out_copy(c):
        span = pl.ds(pl.multiple_of(c * tile, tile), tile)
        return pltpu.make_async_copy(staged.at[c], out.at[:, span], out_sem.at[c])

    def finish(c, carry):
        for copy in near_rows(new_all, new_n, c):
            copy.wait_recv()
        targets = new_all[c].reshape(anchors, tile).astype(F32) * spread_scale[:, :1]
        coeffs = solve(0.125 * D, targets, gram[...].reshape(anchors, anchors))
        top = coeffs.astype(BF16)
        mapped[0] = top
        mapped[1] = (coeffs - top.astype(F32)).astype(BF16)

        @pl.when(c == 0)
        def _():
            for copy in routed_near:
                copy.wait_recv()
            lax.fori_loop(0, n_rows, turn_rows, 0)

        def move(step, inner):
            span = pl.ds(pl.multiple_of(step * row_step, row_step), row_step)
            block = rows_t[span]
            staged[c, span] = (dot(block, mapped[0]) + dot(block, mapped[1])).astype(BF16)
            return inner

        lax.fori_loop(0, n_rows * cap // row_step, move, 0)
        out_copy(c).start()
        return carry

    lax.fori_loop(0, chunks, finish, 0)
    for copy in sent + routed_near:
        copy.wait_send()
    for c in range(chunks):
        for copy in new_near[c]:
            copy.wait_send()
        out_copy(c).wait()


def local(
    hidden, attn_gain, w_query, w_key, w_value, w_output, query_gain, key_gain,
    key_cache, value_cache, lengths, final_gain, old_embed, slab, owners,
):
    n_rows = lax.axis_size("rows")
    n_mp = lax.axis_size("mp")
    docs, width = hidden.shape
    cols = width // n_mp
    anchors = n_rows * docs
    share = anchors // n_mp
    slab_rows = slab.shape[0]
    cap = 2 * slab_rows // n_rows
    kv_width = w_key.shape[1]
    q_width = w_query.shape[1]
    mp_half, rows_half = n_mp // 2, n_rows // 2
    key_cache = key_cache.reshape(-1, kv_width)
    value_cache = value_cache.reshape(-1, kv_width)
    tile = min(256, cols)
    chunks = cols // tile
    far_mp, far_rows = max(mp_half - 1, 1), max(rows_half - 1, 1)
    hbm = pl.BlockSpec(memory_space=pl.ANY)
    dma = pltpu.SemaphoreType.DMA
    return pl.pallas_call(
        functools.partial(encode_kernel, n_mp, n_rows),
        out_shape=jax.ShapeDtypeStruct((n_rows * cap, cols), BF16),
        in_specs=[hbm] * 15,
        out_specs=pl.BlockSpec(memory_space=pl.ANY),
        scratch_shapes=[
            pltpu.VMEM(hidden.shape, BF16),
            pltpu.VMEM((1, width), F32),
            pltpu.VMEM((1, HEAD), F32),
            pltpu.VMEM((1, HEAD), F32),
            pltpu.VMEM((1, docs), jnp.int32),
            pltpu.VMEM((1, width), F32),
            pltpu.VMEM((1, slab_rows), jnp.int32),
            pltpu.VMEM((width, q_width), BF16),
            pltpu.VMEM((width, kv_width), BF16),
            pltpu.VMEM((width, kv_width), BF16),
            pltpu.VMEM((q_width, width), BF16),
            pltpu.VMEM(key_cache.shape, BF16),
            pltpu.VMEM(value_cache.shape, BF16),
            pltpu.VMEM(slab.shape, BF16),
            pltpu.VMEM((docs, width), BF16),
            pltpu.VMEM((docs, q_width), F32),
            pltpu.VMEM((docs, kv_width), F32),
            pltpu.VMEM((docs, kv_width), F32),
            pltpu.VMEM((docs, q_width), BF16),
            pltpu.VMEM((chunks, 2, mp_half, docs, tile), F32),
            pltpu.VMEM((chunks, mp_half, docs, tile), F32),
            pltpu.VMEM((chunks, mp_half, docs, tile), F32),
            pltpu.VMEM((chunks, far_mp, docs, tile), F32),
            pltpu.VMEM((docs, 128), F32),
            pltpu.VMEM((n_mp - 1, docs, 128), F32),
            pltpu.VMEM((n_rows, docs, 128), F32),
            pltpu.VMEM((chunks, n_rows, docs, tile), BF16),
            pltpu.VMEM((n_rows, docs, cols), BF16),
            pltpu.VMEM((2, mp_half, share, slab_rows), F32),
            pltpu.VMEM((mp_half, share, slab_rows), F32),
            pltpu.VMEM((mp_half, share, slab_rows), F32),
            pltpu.VMEM((far_mp, share, slab_rows), F32),
            pltpu.VMEM((2, mp_half, share, anchors), F32),
            pltpu.VMEM((mp_half, share, anchors), F32),
            pltpu.VMEM((mp_half, share, anchors), F32),
            pltpu.VMEM((far_mp, share, anchors), F32),
            pltpu.VMEM((n_rows, share, cap), BF16),
            pltpu.VMEM((n_mp, n_rows, share, cap), BF16),
            pltpu.VMEM((n_mp, share, anchors), F32),
            pltpu.VMEM((docs, 128), F32),
            pltpu.VMEM((anchors, 128), F32),
            pltpu.VMEM((2, anchors, tile), BF16),
            pltpu.VMEM((n_rows * cap, anchors), BF16),
            pltpu.VMEM((n_rows * cap, slab_rows), BF16),
            pltpu.VMEM((chunks, n_rows * cap, tile), BF16),
            dma((11,)), dma((3, CHUNKS)), dma((n_mp * chunks,)),
            dma((2, chunks, 1)), dma((2, chunks, far_mp)), dma((2, n_mp - 1)),
            dma((2, n_rows - 1)),
            dma((2, chunks, far_rows)), dma((2, chunks, rows_half)),
            dma((2, far_rows)), dma((2, rows_half)),
            dma((2, 1)), dma((2, far_mp)),
            dma((2, 1)), dma((2, far_mp)),
            dma((2, n_rows - 1)),
            dma((2, far_mp)), dma((2, mp_half)),
            dma((2, far_mp)), dma((2, mp_half)),
            dma((chunks,)),
        ],
        compiler_params=pltpu.CompilerParams(
            collective_id=0, has_side_effects=True, vmem_limit_bytes=60 * 2**20
        ),
        name="encode",
    )(
        hidden, attn_gain.reshape(1, -1), w_query, w_key, w_value, w_output,
        query_gain.reshape(1, -1), key_gain.reshape(1, -1), key_cache, value_cache,
        lengths.reshape(1, -1), final_gain.reshape(1, -1), old_embed, slab, owners.reshape(1, -1),
    )

def solution(mesh):
    return jax.shard_map(
        local,
        mesh=mesh,
        in_specs=(
            P("rows", None),
            P(),
            P(None, "mp"),
            P(None, "mp"),
            P(None, "mp"),
            P("mp", None),
            P(),
            P(),
            P("rows", None, "mp"),
            P("rows", None, "mp"),
            P("rows"),
            P(),
            P("rows", None),
            P("rows", "mp"),
            P("rows", None),
        ),
        out_specs=P("rows", "mp"),
        check_vma=False,
    )
```

```python
import functools
import math

import jax
import jax.numpy as jnp
from jax import lax
from jax.experimental import pallas as pl
from jax.experimental.pallas import tpu as pltpu
from jax.sharding import PartitionSpec as P

D = 4096
HEADS = 32
KV_HEADS = 8
HEAD = 128
ITERS = 3
MESH = pl.DeviceIdType.MESH
F32 = jnp.float32
BF16 = jnp.bfloat16
CHUNKS = 8


def dot(left, right, left_dim=1, right_dim=0):
    return lax.dot_general(
        left, right, (((left_dim,), (right_dim,)), ((), ())), preferred_element_type=F32
    )


def solve(ridge, start, gram):
    high = gram.astype(BF16)
    low = (gram - high.astype(F32)).astype(BF16)

    def apply(values):
        top = values.astype(BF16)
        rest = (values - top.astype(F32)).astype(BF16)
        return dot(high, top) + (dot(high, rest) + dot(low, top))

    def total(values):
        return jnp.sum(values, axis=0, keepdims=True)

    residual = start
    direction = residual
    image_docs = apply(start)
    res_sq = total(residual * image_docs)
    coeffs = jnp.zeros_like(residual)
    for sweep in range(ITERS):
        curvature = total(image_docs * image_docs) + ridge * total(direction * image_docs)
        alpha = res_sq / curvature
        coeffs = coeffs + alpha * direction
        if sweep + 1 < ITERS:
            residual = residual - alpha * (image_docs + ridge * direction)
            spread = apply(residual)
            new_sq = total(residual * spread)
            ratio = new_sq / res_sq
            direction = residual + ratio * direction
            image_docs = spread + ratio * image_docs
            res_sq = new_sq
    return coeffs


def encode_kernel(
    n_mp, n_rows,
    hidden_in, attn_gain_in, w_query, w_key, w_value, w_output, query_gain_in, key_gain_in,
    key_cache, value_cache, lengths_in, final_gain_in, old_embed, slab, owners_in,
    coeffs_out, rows_out,
    hidden, attn_gain, query_gain, key_gain, lengths, final_gain, owners,
    wq, wk, wv, wo, kc, vc, sl, normed, q_acc, k_acc, v_acc, attended,
    part, part_in, part_sum, part_far, sq_own, sq_in, scale_all, new_all,
    old_all, side, side_in, side_sum, side_far, pair, pair_in, pair_sum, pair_far,
    outgoing, routed, gram, spread_scale, mapped, rows_t, puts,
    load_sem, weight_sem, wo_sem,
    part_a, part_b, sq_sem, scale_sem, new_f, new_n, old_d,
    side_a, side_b, pair_a, pair_b,
    trip_sem, gram_f, gram_n, routed_f, routed_n, out_sem,
):
    mp = lax.axis_index("mp")
    row = lax.axis_index("rows")
    docs, width = hidden.shape
    cols = width // n_mp
    anchors = n_rows * docs
    share = anchors // n_mp
    slab_rows = slab.shape[0]
    cap = outgoing.shape[2]
    chunks, tile = new_all.shape[0], new_all.shape[3]
    kv_local = k_acc.shape[1] // HEAD
    group = HEADS // KV_HEADS
    ctx = key_cache.shape[0] // docs
    mp_half, rows_half = n_mp // 2, n_rows // 2
    mp_slow, core = mp // 2, mp % 2
    row_slow, row_fast = row // 2, row % 2

    def remote(src, dst, sems, spot, to_mp, to_row):
        spot = spot if isinstance(spot, tuple) else (spot,)
        return pltpu.make_async_remote_copy(
            src_ref=src, dst_ref=dst, send_sem=sems.at[(0, *spot)],
            recv_sem=sems.at[(1, *spot)],
            device_id={"mp": to_mp, "rows": to_row}, device_id_type=MESH,
        )

    def far_rows(buf, sems, *lead):
        return [
            remote(buf.at[(*lead, row)], buf.at[(*lead, row)], sems, (*lead, off - 1), mp,
                   ((row_slow + off) % rows_half) * 2 + row_fast)
            for off in range(1, rows_half)
        ]

    def near_rows(buf, sems, *lead):
        found = []
        for off in range(rows_half):
            block = ((row_slow + rows_half - off) % rows_half) * 2 + row_fast
            found.append(remote(buf.at[(*lead, block)], buf.at[(*lead, block)], sems,
                                (*lead, off), mp, row_slow * 2 + 1 - row_fast))
        return found

    def far_mp(buf, sems):
        return [
            remote(buf.at[mp], buf.at[mp], sems, off - 1,
                   ((mp_slow + off) % mp_half) * 2 + core, row)
            for off in range(1, mp_half)
        ]

    def near_mp(buf, sems):
        found = []
        for off in range(mp_half):
            block = ((mp_slow + mp_half - off) % mp_half) * 2 + core
            found.append(remote(buf.at[block], buf.at[block], sems, off,
                                mp_slow * 2 + 1 - core, row))
        return found

    def reduce_near(partial, landed, sems, *lead):
        return remote(partial.at[(*lead, 1 - core)], landed.at[lead] if lead else landed, sems,
                      (*lead, 0), mp_slow * 2 + 1 - core, row)

    def reduce_far(summed, landed, sems, *lead):
        found = []
        for off in range(1, mp_half):
            there = (mp_slow + off) % mp_half
            found.append(remote(summed.at[(*lead, there)], landed.at[(*lead, off - 1)], sems,
                                (*lead, off - 1), there * 2 + core, row))
        return found

    def start(copies):
        for copy in copies:
            copy.start()

    sent = []

    def received(copies):
        for copy in copies:
            copy.wait_recv()
            sent.append(copy)

    depth = width // CHUNKS

    def weight_copies(step):
        span = pl.ds(pl.multiple_of(step * depth, depth), depth)
        return [
            pltpu.make_async_copy(src.at[span, :], dst.at[span, :], weight_sem.at[i, step])
            for i, (src, dst) in enumerate(((w_query, wq), (w_key, wk), (w_value, wv)))
        ]

    def output_block(step):
        step = step % n_mp
        return 2 * (step % mp_half) + lax.rem(core + 1 + step // mp_half, 2)

    def output_span(step):
        base = output_block(step) * cols + step // n_mp * tile
        return pl.ds(pl.multiple_of(base, tile), tile)

    def output_copy(step):
        span = output_span(step)
        return pltpu.make_async_copy(w_output.at[:, span], wo.at[:, span], wo_sem.at[step])

    barrier = pltpu.get_barrier_semaphore()
    for off in range(1, n_rows):
        pl.semaphore_signal(barrier, inc=1, device_id={"mp": mp, "rows": lax.rem(row + off, n_rows)},
                            device_id_type=MESH)
    for off in range(1, n_mp):
        pl.semaphore_signal(barrier, inc=1, device_id={"mp": lax.rem(mp + off, n_mp), "rows": row},
                            device_id_type=MESH)
    mine = pl.ds(pl.multiple_of(mp * cols, cols), cols)
    loads = [
        pltpu.make_async_copy(src, dst, load_sem.at[i])
        for i, (src, dst) in enumerate((
            (key_cache, kc), (value_cache, vc), (slab, sl),
            (hidden_in, hidden), (attn_gain_in, attn_gain),
            (old_embed.at[:, mine], old_all.at[row]), (owners_in, owners),
            (lengths_in, lengths), (query_gain_in, query_gain), (key_gain_in, key_gain),
            (final_gain_in, final_gain),
        ))
    ]
    start(loads[3:])
    for step in range(CHUNKS):
        start(weight_copies(step))
    start(loads[:3])
    for step in range(n_mp * chunks):
        output_copy(step).start()

    loads[3].wait()
    loads[4].wait()
    hidden32 = hidden[...].astype(F32)
    normed[...] = (
        hidden32 * lax.rsqrt(jnp.mean(hidden32 * hidden32, axis=-1, keepdims=True) + 1e-06)
        * attn_gain[...]
    ).astype(BF16)
    for copy in loads[5:]:
        copy.wait()
    pl.semaphore_wait(barrier, n_rows + n_mp - 2)

    old_direct = [
        remote(old_all.at[row], old_all.at[row], old_d, off - 1, mp, lax.rem(row + off, n_rows))
        for off in range(1, n_rows)
    ]
    start(old_direct)

    q_acc[...] = jnp.zeros_like(q_acc)
    k_acc[...] = jnp.zeros_like(k_acc)
    v_acc[...] = jnp.zeros_like(v_acc)

    owner = owners[...]
    chosen = jnp.where(
        owner == lax.broadcasted_iota(jnp.int32, (n_rows, slab_rows), 0), 1.0, 0.0
    )
    earlier = jnp.where(
        lax.broadcasted_iota(jnp.int32, (slab_rows, slab_rows), 0)
        < lax.broadcasted_iota(jnp.int32, (slab_rows, slab_rows), 1), 1.0, 0.0
    )
    slot = jnp.sum(
        dot(chosen.astype(BF16), earlier.astype(BF16)) * chosen, axis=0, keepdims=True
    )
    target = owner.astype(F32) * cap + slot
    seats = lax.broadcasted_iota(jnp.int32, (cap, slab_rows), 0).astype(F32)

    def put(o, carry):
        base = (o * cap).astype(F32)
        puts[pl.ds(pl.multiple_of(o * cap, cap), cap)] = jnp.where(
            target - base == seats, 1.0, 0.0
        ).astype(BF16)
        return carry

    lax.fori_loop(0, n_rows, put, 0)

    def project(step, carry):
        span = pl.ds(pl.multiple_of(step * depth, depth), depth)
        for copy in weight_copies(step):
            copy.wait()
        piece = normed[:, span]
        q_acc[...] += dot(piece, wq[span, :])
        k_acc[...] += dot(piece, wk[span, :])
        v_acc[...] += dot(piece, wv[span, :])
        return carry

    lax.fori_loop(0, CHUNKS, project, 0)

    spot = lax.broadcasted_iota(jnp.int32, (docs, docs), 0)
    named = lax.broadcasted_iota(jnp.int32, (docs, docs), 1)
    length = jnp.sum(
        jnp.where(spot == named, lengths[...].astype(F32), 0.0), axis=-1, keepdims=True
    )
    lane = lax.broadcasted_iota(jnp.int32, (docs, HEAD), 1)
    half = HEAD // 2
    frequency = jnp.exp(
        -(2.0 * (lane % half).astype(F32) / HEAD) * math.log(1000000.0)
    )
    angle = length * frequency
    cosine = jnp.cos(angle)
    sine = jnp.sin(angle) * jnp.where(lane < half, -1.0, 1.0)

    def turned(values, gain):
        scale = lax.rsqrt(jnp.mean(values * values, axis=-1, keepdims=True) + 1e-06)
        values = values * scale * gain
        return values * cosine + pltpu.roll(values, half, 1) * sine

    loads[0].wait()
    loads[1].wait()
    few = min(8, docs)
    tall, wide = group * few, few * ctx
    place_row = lax.broadcasted_iota(jnp.int32, (tall, wide), 0) % few * ctx
    place_lane = lax.broadcasted_iota(jnp.int32, (tall, wide), 1)
    factor = 1.0 / math.sqrt(HEAD)
    for g in range(kv_local):
        span = slice(g * HEAD, (g + 1) * HEAD)
        queries = [
            turned(q_acc[:, (g * group + h) * HEAD:(g * group + h + 1) * HEAD], query_gain[...])
            for h in range(group)
        ]
        key_new = turned(k_acc[:, span], key_gain[...]).astype(BF16).astype(F32)
        value_new = v_acc[:, span].astype(BF16).astype(F32)
        mixed = []
        for first in range(0, docs, few):
            some = slice(first, first + few)
            ask = jnp.concatenate([query[some] for query in queries], axis=0).astype(BF16)
            long = jnp.concatenate([length[some]] * group, axis=0).astype(jnp.int32)
            valid = (place_lane >= place_row) & (place_lane < place_row + long)
            held = slice(first * ctx, (first + few) * ctx)
            scores = jnp.where(valid, dot(ask, kc[held, span], 1, 1) * factor, -jnp.inf)
            own_score = jnp.sum(
                ask.astype(F32) * jnp.concatenate([key_new[some]] * group, axis=0),
                axis=-1, keepdims=True,
            ) * factor
            top = jnp.maximum(jnp.max(scores, axis=-1, keepdims=True), own_score)
            expo = jnp.exp(scores - top)
            own_expo = jnp.exp(own_score - top)
            inverse = 1.0 / (jnp.sum(expo, axis=-1, keepdims=True) + own_expo)
            weights = (expo * inverse).astype(BF16)
            own_weight = (own_expo * inverse).astype(BF16).astype(F32)
            mixed.append(
                dot(weights, vc[held, span])
                + own_weight * jnp.concatenate([value_new[some]] * group, axis=0)
            )
        for h in range(group):
            attended[:, (g * group + h) * HEAD:(g * group + h + 1) * HEAD] = jnp.concatenate(
                [block[h * few:(h + 1) * few] for block in mixed], axis=0
            ).astype(BF16)

    def project_out(step, carry):
        output_copy(step).wait()
        block = output_block(step)
        part[step // n_mp, block % 2, block // 2] = dot(attended[...], wo[:, output_span(step)])
        return carry

    part_near = [reduce_near(part, part_in, part_a, c) for c in range(chunks)]
    part_apart = [reduce_far(part_sum, part_far, part_b, c) for c in range(chunks)]
    width_step = min(256, anchors, slab_rows)

    def multiply(into, right):
        def piece(step, carry):
            span = pl.ds(pl.multiple_of(step * width_step, width_step), width_step)
            product = dot(old_all[...].reshape(anchors, cols), right(span), 1, 1)
            for j in range(n_mp):
                into[j % 2, j // 2, :, span] = product[j * share:(j + 1) * share]
            return carry

        lax.fori_loop(0, into.shape[3] // width_step, piece, 0)

    def add_near(c):
        received([part_near[c]])
        part_sum[c] = part[c, core] + part_in[c]
        start(part_apart[c])

    side_near = reduce_near(side, side_in, side_a)
    side_apart = reduce_far(side_sum, side_far, side_b)
    pair_near = reduce_near(pair, pair_in, pair_a)
    pair_apart = reduce_far(pair_sum, pair_far, pair_b)
    for c in range(chunks):
        lax.fori_loop(c * n_mp, c * n_mp + mp_half, project_out, 0)
        part_near[c].start()
        lax.fori_loop(c * n_mp + mp_half, (c + 1) * n_mp, project_out, 0)
        if c:
            add_near(c - 1)
    add_near(chunks - 1)
    received(old_direct)
    loads[2].wait()
    multiply(side, lambda span: sl[span])
    side_near.start()
    docs_step = width_step // docs
    multiply(
        pair,
        lambda span: old_all[pl.ds(span.start // docs, docs_step)].reshape(width_step, cols),
    )
    pair_near.start()
    received([side_near])
    side_sum[...] = side[core] + side_in[...]
    start(side_apart)

    new_far = [far_rows(new_all, new_f, c) for c in range(chunks)]
    new_near = [near_rows(new_all, new_n, c) for c in range(chunks)]
    square = jnp.zeros((docs, 1), F32)
    for c in range(chunks):
        received(part_apart[c])
        span = pl.ds(pl.multiple_of(mp * cols + c * tile, tile), tile)
        state = hidden[:, span].astype(F32) + part_sum[c, mp_slow]
        for off in range(1, mp_half):
            state = state + part_far[c, off - 1]
        new_all[c, row] = (state * final_gain[:, span]).astype(BF16)
        start(new_far[c])
        new_near[c][0].start()
        square = square + jnp.sum(state * state, axis=-1, keepdims=True)
    sq_own[...] = jnp.broadcast_to(square, sq_own.shape)
    sq_copies = [
        remote(sq_own, sq_in.at[off - 1], sq_sem, off - 1, lax.rem(mp + off, n_mp), row)
        for off in range(1, n_mp)
    ]
    start(sq_copies)

    received(side_apart)
    whole = side_sum[mp_slow]
    for off in range(1, mp_half):
        whole = whole + side_far[off - 1]
    body = whole.astype(BF16)

    for o in range(n_rows):
        outgoing[o] = dot(body, puts[o * cap:(o + 1) * cap], 1, 1).astype(BF16)
    trips = []
    for off in range(1, n_rows):
        there = lax.rem(row + off, n_rows)
        trips.append(remote(outgoing.at[there], routed.at[mp, row], trip_sem, off - 1, mp, there))
    start(trips)
    routed[mp, row] = outgoing[row]

    received(sq_copies)
    total = sq_own[...]
    for off in range(1, n_mp):
        total = total + sq_in[off - 1]
    scale_all[row] = lax.rsqrt(total / width + 1e-06)
    scale_copies = [
        remote(scale_all.at[row], scale_all.at[row], scale_sem, off - 1, mp,
               lax.rem(row + off, n_rows))
        for off in range(1, n_rows)
    ]
    start(scale_copies)

    received([pair_near])
    pair_sum[...] = pair[core] + pair_in[...]
    start(pair_apart)

    def forward(c):
        received(new_far[c])
        start(new_near[c][1:])

    for c in range(chunks // 2):
        forward(c)
    received(trips)
    routed_far = far_mp(routed, routed_f)
    start(routed_far)
    routed_near = near_mp(routed, routed_n)
    routed_near[0].start()
    received(pair_apart)
    whole = pair_sum[mp_slow]
    for off in range(1, mp_half):
        whole = whole + pair_far[off - 1]
    gram[mp] = whole
    gram_far = far_mp(gram, gram_f)
    start(gram_far)
    gram_near = near_mp(gram, gram_n)
    gram_near[0].start()

    for c in range(chunks // 2, chunks):
        forward(c)
    received(routed_far)
    start(routed_near[1:])
    received(gram_far)
    start(gram_near[1:])

    received(gram_near)
    received(scale_copies)
    scale = scale_all[...].reshape(anchors, HEAD)[:, :1]
    spread_scale[...] = jnp.broadcast_to(scale, spread_scale.shape)
    rows_copy = pltpu.make_async_copy(rows_t, rows_out, out_sem.at[chunks])

    def turn_rows(b, carry):
        span = pl.ds(pl.multiple_of(b * cap, cap), cap)
        rows_t[span] = routed[:, b].reshape(anchors, cap).T
        return carry

    def coeffs_copy(c):
        return pltpu.make_async_copy(mapped.at[c], coeffs_out.at[c], out_sem.at[c])

    def finish(c, carry):
        @pl.when(c == chunks - 1)
        def _():
            for copy in routed_near:
                copy.wait_recv()
            lax.fori_loop(0, n_rows, turn_rows, 0)
            rows_copy.start()

        for copy in near_rows(new_all, new_n, c):
            copy.wait_recv()
        targets = new_all[c].reshape(anchors, tile).astype(F32) * spread_scale[:, :1]
        coeffs = solve(0.125 * D, targets, gram[...].reshape(anchors, anchors))
        top = coeffs.astype(BF16)
        mapped[c, 0] = top
        mapped[c, 1] = (coeffs - top.astype(F32)).astype(BF16)
        coeffs_copy(c).start()
        return carry

    lax.fori_loop(0, chunks, finish, 0)
    for copy in sent + routed_near:
        copy.wait_send()
    for c in range(chunks):
        for copy in new_near[c]:
            copy.wait_send()
        coeffs_copy(c).wait()
    rows_copy.wait()


def apply_kernel(rows, coeffs, out):
    out[...] = (dot(rows[...], coeffs[0, 0]) + dot(rows[...], coeffs[0, 1])).astype(BF16)


def local(
    hidden, attn_gain, w_query, w_key, w_value, w_output, query_gain, key_gain,
    key_cache, value_cache, lengths, final_gain, old_embed, slab, owners,
):
    n_rows = lax.axis_size("rows")
    n_mp = lax.axis_size("mp")
    docs, width = hidden.shape
    cols = width // n_mp
    anchors = n_rows * docs
    share = anchors // n_mp
    slab_rows = slab.shape[0]
    cap = 2 * slab_rows // n_rows
    kv_width = w_key.shape[1]
    q_width = w_query.shape[1]
    mp_half, rows_half = n_mp // 2, n_rows // 2
    key_cache = key_cache.reshape(-1, kv_width)
    value_cache = value_cache.reshape(-1, kv_width)
    tile = min(256, cols)
    chunks = cols // tile
    far_mp, far_rows = max(mp_half - 1, 1), max(rows_half - 1, 1)
    hbm = pl.BlockSpec(memory_space=pl.ANY)
    dma = pltpu.SemaphoreType.DMA
    coeffs, rows = pl.pallas_call(
        functools.partial(encode_kernel, n_mp, n_rows),
        out_shape=(
            jax.ShapeDtypeStruct((chunks, 2, anchors, tile), BF16),
            jax.ShapeDtypeStruct((n_rows * cap, anchors), BF16),
        ),
        in_specs=[hbm] * 15,
        out_specs=(hbm, hbm),
        scratch_shapes=[
            pltpu.VMEM(hidden.shape, BF16),
            pltpu.VMEM((1, width), F32),
            pltpu.VMEM((1, HEAD), F32),
            pltpu.VMEM((1, HEAD), F32),
            pltpu.VMEM((1, docs), jnp.int32),
            pltpu.VMEM((1, width), F32),
            pltpu.VMEM((1, slab_rows), jnp.int32),
            pltpu.VMEM((width, q_width), BF16),
            pltpu.VMEM((width, kv_width), BF16),
            pltpu.VMEM((width, kv_width), BF16),
            pltpu.VMEM((q_width, width), BF16),
            pltpu.VMEM(key_cache.shape, BF16),
            pltpu.VMEM(value_cache.shape, BF16),
            pltpu.VMEM(slab.shape, BF16),
            pltpu.VMEM((docs, width), BF16),
            pltpu.VMEM((docs, q_width), F32),
            pltpu.VMEM((docs, kv_width), F32),
            pltpu.VMEM((docs, kv_width), F32),
            pltpu.VMEM((docs, q_width), BF16),
            pltpu.VMEM((chunks, 2, mp_half, docs, tile), F32),
            pltpu.VMEM((chunks, mp_half, docs, tile), F32),
            pltpu.VMEM((chunks, mp_half, docs, tile), F32),
            pltpu.VMEM((chunks, far_mp, docs, tile), F32),
            pltpu.VMEM((docs, 128), F32),
            pltpu.VMEM((n_mp - 1, docs, 128), F32),
            pltpu.VMEM((n_rows, docs, 128), F32),
            pltpu.VMEM((chunks, n_rows, docs, tile), BF16),
            pltpu.VMEM((n_rows, docs, cols), BF16),
            pltpu.VMEM((2, mp_half, share, slab_rows), F32),
            pltpu.VMEM((mp_half, share, slab_rows), F32),
            pltpu.VMEM((mp_half, share, slab_rows), F32),
            pltpu.VMEM((far_mp, share, slab_rows), F32),
            pltpu.VMEM((2, mp_half, share, anchors), F32),
            pltpu.VMEM((mp_half, share, anchors), F32),
            pltpu.VMEM((mp_half, share, anchors), F32),
            pltpu.VMEM((far_mp, share, anchors), F32),
            pltpu.VMEM((n_rows, share, cap), BF16),
            pltpu.VMEM((n_mp, n_rows, share, cap), BF16),
            pltpu.VMEM((n_mp, share, anchors), F32),
            pltpu.VMEM((anchors, 128), F32),
            pltpu.VMEM((chunks, 2, anchors, tile), BF16),
            pltpu.VMEM((n_rows * cap, anchors), BF16),
            pltpu.VMEM((n_rows * cap, slab_rows), BF16),
            dma((11,)), dma((3, CHUNKS)), dma((n_mp * chunks,)),
            dma((2, chunks, 1)), dma((2, chunks, far_mp)), dma((2, n_mp - 1)),
            dma((2, n_rows - 1)),
            dma((2, chunks, far_rows)), dma((2, chunks, rows_half)),
            dma((2, n_rows - 1)),
            dma((2, 1)), dma((2, far_mp)),
            dma((2, 1)), dma((2, far_mp)),
            dma((2, n_rows - 1)),
            dma((2, far_mp)), dma((2, mp_half)),
            dma((2, far_mp)), dma((2, mp_half)),
            dma((chunks + 1,)),
        ],
        compiler_params=pltpu.CompilerParams(
            collective_id=0, has_side_effects=True, vmem_limit_bytes=60 * 2**20
        ),
        name="encode",
    )(
        hidden, attn_gain.reshape(1, -1), w_query, w_key, w_value, w_output,
        query_gain.reshape(1, -1), key_gain.reshape(1, -1), key_cache, value_cache,
        lengths.reshape(1, -1), final_gain.reshape(1, -1), old_embed, slab, owners.reshape(1, -1),
    )
    return pl.pallas_call(
        apply_kernel,
        out_shape=jax.ShapeDtypeStruct((n_rows * cap, cols), BF16),
        grid=(chunks,),
        in_specs=[
            pl.BlockSpec((n_rows * cap, anchors), lambda i: (0, 0)),
            pl.BlockSpec((1, 2, anchors, tile), lambda i: (i, 0, 0, 0)),
        ],
        out_specs=pl.BlockSpec((n_rows * cap, tile), lambda i: (0, i)),
        compiler_params=pltpu.CompilerParams(vmem_limit_bytes=60 * 2**20),
        name="apply",
    )(rows, coeffs)

def solution(mesh):
    return jax.shard_map(
        local,
        mesh=mesh,
        in_specs=(
            P("rows", None),
            P(),
            P(None, "mp"),
            P(None, "mp"),
            P(None, "mp"),
            P("mp", None),
            P(),
            P(),
            P("rows", None, "mp"),
            P("rows", None, "mp"),
            P("rows"),
            P(),
            P("rows", None),
            P("rows", "mp"),
            P("rows", None),
        ),
        out_specs=P("rows", "mp"),
        check_vma=False,
    )
```
